32 devices in a mesh: scan: 2 (over y), slab: 4 (over z), coil: 4 (over x, core).
Axes of the slice: x: 2, y: 2, z: 4, core: 2. Of those that a mesh axis runs over, the one named last changes fastest.
Arguments:
- coil_maps: float32 [16, 4, 2, 384, 384], P('coil', 'scan', None, 'slab'), parts along dimension 1, may hold values from -5 to 5
- samples: float32 [16, 4, 1024, 128], P('coil', 'scan', 'slab'), parts along dimension 1, may hold values from -6 to 6
- kernel: float32 [128, 128], replicated, may hold values from -2 to 3
- tile_block: int32 [1024], P('slab'), may hold values from 0 to 575
- tile_count: int32 [1024], P('slab'), may hold values from 32 to 128
- dcf_level: int32 [1024], P('slab'), may hold values from 0 to 15
- dcf_table: float32 [16], replicated, may hold values from 0.2 to 5
Outputs:
- solution: float32 [4, 2, 384, 384], P('scan', None, 'slab'), parts along dimension 0
- residual: float32 [4, 2, 384, 384], P('scan', None, 'slab'), parts along dimension 0
The draws below stay inside these ranges and needn't reach their ends.
There are 2 independent parts, one for each index of `scan`. The reference program is written for one: setup_inputs(seed, part) draws one part's arguments, and reference() takes and returns one part's arrays. A program takes and returns all parts, laid end to end along the dimension named above; an argument that names none is the same for every part. Nothing has to cross between parts.
All inputs are finite; a program needn't handle non-finite values.
Results may differ from the reference program's by a relative error of at most 0.00018.
Values sent between devices are 32-bit elements; how exact they have to be, the bound alone decides.
A program may use at most 128 MiB of HBM per device.

```python
import math
import jax
import jax.numpy as jnp
from jax import lax

NC = 16
NY = 384
NZ = 384
BLOCK = 128
LEVELS = 16
ITERS = 2
XPOS = 2
TPD = 256
TILES = 1024
BPD = 576
N_SLAB = 4


def draw_kernel(key, part):
    key = jax.random.fold_in(key, 7)
    index = jnp.arange(BLOCK, dtype=jnp.int32)
    diagonal = (index[:, None] == index[None, :]).astype(jnp.float32)
    noise = jnp.clip(jax.random.normal(key, (BLOCK, BLOCK), jnp.float32), -4.0, 4.0)
    return diagonal + 0.5 * noise / jnp.sqrt(jnp.float32(BLOCK))


def with_ends(drawn, rng, low, largest):
    spot = [jax.random.randint(jax.random.fold_in(rng, axis), (), 0, length) for axis, length in enumerate(drawn.shape)]
    main_axis = drawn.shape.index(max(drawn.shape))
    next_to = spot[:main_axis] + [(spot[main_axis] + 1) % drawn.shape[main_axis]] + spot[main_axis + 1:]
    return drawn.at[tuple(spot)].set(low).at[tuple(next_to)].set(largest)


def block_levels(rng, extent, cuts, low, largest):
    gain, own = 1.0, jax.random.fold_in(rng, 6)
    for position, shards_of in cuts:
        draws = jnp.exp(jax.random.uniform(jax.random.fold_in(own, position), (shards_of,), jnp.float32, low / len(cuts), largest / len(cuts)))
        gain = gain * jnp.repeat(draws, extent[position] // shards_of).reshape([-1 if axis == position else 1 for axis in range(len(extent))])
    return gain


def centred(own_key, shape, width, limit, shards=(), kind=jnp.bfloat16):
    array = width * jax.random.normal(own_key, shape, jnp.float32)
    if shards:
        array = array * block_levels(own_key, shape, shards, -0.22, 0.18)
    return jnp.clip(array, -limit, limit).astype(kind)


def setup_inputs(seed: int = 0, part: int = 0) -> dict:
    key_list = jax.random.split(jax.random.key(seed), 8)
    own_keys = jax.random.split(jax.random.fold_in(key_list[7], part), 8)
    return {
        "coil_maps": centred(own_keys[0], (NC, 2, XPOS, NZ, NY), 0.35, 5.0, ((0, 4), (3, 4)), jnp.float32),
        "samples": centred(own_keys[1], (NC, 2, TILES, BLOCK), 1.0, 6.0, ((0, 4), (2, 4)), jnp.float32),
        "kernel": draw_kernel(jax.random.fold_in(key_list[7], 71), part),
        "tile_block": with_ends(jax.random.randint(key_list[3], (TILES,), 0, BPD), jax.random.fold_in(key_list[3], 1), 0, BPD - 1).astype(jnp.int32),
        "tile_count": with_ends(jax.random.randint(key_list[4], (TILES,), BLOCK // 4, BLOCK + 1), jax.random.fold_in(key_list[4], 1), BLOCK // 4, BLOCK).astype(jnp.int32),
        "dcf_level": with_ends(jax.random.randint(key_list[5], (TILES,), 0, LEVELS), jax.random.fold_in(key_list[5], 1), 0, LEVELS - 1).astype(jnp.int32),
        "dcf_table": jnp.clip(jnp.exp(jax.random.uniform(key_list[6], (LEVELS,), jnp.float32, math.log(0.2), math.log(5.0))), 0.2, 5.0),
    }


HIGH = lax.Precision.HIGHEST
SHIFT = 0.5

def tables(count):
    index = jnp.arange(count, dtype=jnp.int32)
    phase = index[:, None] * index[None, :] % count
    angle = phase.astype(jnp.float32) * (2.0 * math.pi / count)
    factor = 1.0 / math.sqrt(count)
    return (jnp.cos(angle) * factor, jnp.sin(angle) * factor)

def transform(real, imag, cosine, sine, sign, form):
    rc = jnp.einsum(form, real, cosine, precision=HIGH)
    rs = jnp.einsum(form, real, sine, precision=HIGH)
    mc = jnp.einsum(form, imag, cosine, precision=HIGH)
    ms = jnp.einsum(form, imag, sine, precision=HIGH)
    return (rc - sign * ms, mc + sign * rs)

def reference(coil_maps, samples, kernel, tile_block, tile_count, dcf_level, dcf_table):
    ky_dev = NY // N_SLAB
    zblocks = NZ // BLOCK
    cos_y, sin_y = tables(NY)
    cos_z, sin_z = tables(NZ)
    levels = jnp.arange(LEVELS, dtype=jnp.int32)
    density = lax.optimization_barrier(jnp.sum(jnp.where(dcf_level[:, None] == levels[None, :], dcf_table[None, :], 0.0), axis=1))
    valid = (jnp.arange(BLOCK, dtype=jnp.int32)[None, :] < tile_count[:, None]).astype(jnp.float32)
    weight = density[:, None] * valid
    owner = jnp.arange(TILES, dtype=jnp.int32) // TPD * BPD + tile_block

    def to_blocks(grid):
        grid = grid.reshape(XPOS, N_SLAB, ky_dev, zblocks, BLOCK).transpose(1, 0, 2, 3, 4)
        return grid.reshape(N_SLAB * BPD, BLOCK)

    def from_blocks(blocks):
        blocks = blocks.reshape(N_SLAB, XPOS, ky_dev, zblocks, BLOCK).transpose(1, 0, 2, 3, 4)
        return blocks.reshape(XPOS, NY, NZ)

    def sample_one(maps, image):
        map_r, map_i = (maps[0], maps[1])
        coil_r = map_r * image[0] - map_i * image[1]
        coil_i = map_r * image[1] + map_i * image[0]
        spec_r, spec_i = transform(coil_r, coil_i, cos_y, sin_y, -1.0, 'xzn,nk->xzk')
        grid_r, grid_i = transform(spec_r, spec_i, cos_z, sin_z, -1.0, 'xzy,zk->xyk')
        pick_r = to_blocks(grid_r)[owner]
        pick_i = to_blocks(grid_i)[owner]
        out_r = jnp.dot(pick_r, kernel.T, precision=HIGH) * weight
        out_i = jnp.dot(pick_i, kernel.T, precision=HIGH) * weight
        return (out_r, out_i)

    def adjoint_one(maps, values_r, values_i):
        back_r = jnp.dot(values_r, kernel, precision=HIGH)
        back_i = jnp.dot(values_i, kernel, precision=HIGH)
        blank = jnp.zeros((N_SLAB * BPD, BLOCK), jnp.float32)
        grid_r = from_blocks(blank.at[owner].add(back_r))
        grid_i = from_blocks(blank.at[owner].add(back_i))
        spec_r, spec_i = transform(grid_r, grid_i, cos_z, sin_z, 1.0, 'xyk,zk->xzy')
        coil_r, coil_i = transform(spec_r, spec_i, cos_y, sin_y, 1.0, 'xzn,nk->xzk')
        map_r, map_i = (maps[0], maps[1])
        return jnp.stack((map_r * coil_r + map_i * coil_i, map_r * coil_i - map_i * coil_r), 0)

    def rhs_one(pair):
        maps, data = pair
        return adjoint_one(maps, data[0] * weight, data[1] * weight)

    def apply(image):

        def normal_one(maps):
            out_r, out_i = sample_one(maps, image)
            return adjoint_one(maps, out_r, out_i)
        return lax.optimization_barrier(jnp.sum(lax.map(normal_one, coil_maps), axis=0)) + SHIFT * image
    rhs = lax.optimization_barrier(jnp.sum(lax.map(rhs_one, (coil_maps, samples)), axis=0))
    solution = jnp.zeros_like(rhs)
    residual = rhs
    direction = rhs
    norm_now = jnp.sum(residual * residual)
    for step in range(ITERS):
        image = apply(direction)
        alpha = norm_now / jnp.sum(direction * image)
        solution = solution + alpha * direction
        residual = residual - alpha * image
        norm_next = jnp.sum(residual * residual)
        direction = residual + norm_next / norm_now * direction
        norm_now = norm_next
    return (solution, residual)
```

```python
import math

import jax
import jax.numpy as jnp
import ml_dtypes
import numpy as np
from jax import lax
from jax.experimental import pallas as pl
from jax.experimental.pallas import tpu as pltpu
from jax.sharding import PartitionSpec as P

ITERS = 2


HIGH = lax.Precision.HIGHEST
SHIFT = 0.5


def tables(count):
    index = jnp.arange(count, dtype=jnp.int32)
    phase = index[:, None] * index[None, :] % count
    angle = phase.astype(jnp.float32) * (2.0 * math.pi / count)
    factor = 1.0 / math.sqrt(count)
    return (jnp.cos(angle) * factor, jnp.sin(angle) * factor)


def transform(real, imag, cosine, sine, sign, form):
    rc = jnp.einsum(form, real, cosine, precision=HIGH)
    rs = jnp.einsum(form, real, sine, precision=HIGH)
    mc = jnp.einsum(form, imag, cosine, precision=HIGH)
    ms = jnp.einsum(form, imag, sine, precision=HIGH)
    return (rc - sign * ms, mc + sign * rs)


def body(coil_maps, samples, kernel, tile_block, tile_count, dcf_level, dcf_table):
    ncoil, _, xpos, zdev, ylen = coil_maps.shape
    blocklen = kernel.shape[0]
    slabs = lax.axis_size("slab")
    zlen = zdev * slabs
    ky_dev = ylen // slabs
    nblocks = xpos * ky_dev * (zlen // blocklen)
    cos_y, sin_y = tables(ylen)
    cos_z, sin_z = tables(zlen)
    levels = jnp.arange(dcf_table.shape[0], dtype=jnp.int32)
    density = jnp.sum(
        jnp.where(dcf_level[:, None] == levels[None, :], dcf_table[None, :], 0.0), axis=1
    )
    valid = (jnp.arange(blocklen, dtype=jnp.int32)[None, :] < tile_count[:, None]).astype(
        jnp.float32
    )
    weight = density[:, None] * valid
    map_r = coil_maps[:, 0]
    map_i = coil_maps[:, 1]

    def inverse_y(piece):
        out_r, out_i = transform(piece[:, 0], piece[:, 1], cos_y, sin_y, 1.0, "cxzn,nk->cxzk")
        return jnp.stack((out_r, out_i), 1)

    def to_image(values):
        back = jnp.einsum("cita,ab->citb", values, kernel, precision=HIGH)
        blank = jnp.zeros((ncoil, 2, nblocks, blocklen), jnp.float32)
        grid = blank.at[:, :, tile_block].add(back).reshape(ncoil, 2, xpos, ky_dev, zlen)
        part_r, part_i = transform(grid[:, 0], grid[:, 1], cos_z, sin_z, 1.0, "cxyk,zk->cxzy")
        spectra = jnp.stack((part_r, part_i), 1)
        coils = inverse_y(lax.all_to_all(spectra, "slab", split_axis=3, concat_axis=4, tiled=True))
        coil_r = coils[:, 0]
        coil_i = coils[:, 1]
        sum_r = jnp.sum(map_r * coil_r + map_i * coil_i, axis=0)
        sum_i = jnp.sum(map_r * coil_i - map_i * coil_r, axis=0)
        return jnp.stack((sum_r, sum_i), 0)

    rhs_local = to_image(samples * weight)

    def total(local):
        return lax.psum(local, "coil")

    def inner(first, second):
        return lax.psum(jnp.sum(first * second), "slab")

    rhs = total(rhs_local)
    solution = jnp.zeros_like(rhs)
    residual = rhs
    direction = rhs
    norm_now = inner(residual, residual)
    for step in range(ITERS):
        sample_coil_r = map_r * direction[0][None] - map_i * direction[1][None]
        sample_coil_i = map_r * direction[1][None] + map_i * direction[0][None]
        spec_r, spec_i = transform(
            sample_coil_r, sample_coil_i, cos_y, sin_y, -1.0, "cxzn,nk->cxzk"
        )
        sample_spectra = jnp.stack((spec_r, spec_i), 1)
        forward_piece = lax.all_to_all(
            sample_spectra, "slab", split_axis=4, concat_axis=3, tiled=True
        )
        forward_out_r, forward_out_i = transform(
            forward_piece[:, 0], forward_piece[:, 1], cos_z, sin_z, -1.0, "cxzy,zk->cxyk"
        )
        sample_grid = jnp.stack((forward_out_r, forward_out_i), 1)
        blocks = sample_grid.reshape(ncoil, 2, nblocks, blocklen)
        picked = blocks[:, :, tile_block]
        image = (
            total(to_image(jnp.einsum("citb,ab->cita", picked, kernel, precision=HIGH) * weight))
            + SHIFT * direction
        )
        alpha = norm_now / inner(direction, image)
        solution = solution + alpha * direction
        residual = residual - alpha * image
        norm_next = inner(residual, residual)
        direction = residual + norm_next / norm_now * direction
        norm_now = norm_next
    return (solution, residual)


RADIX = 3
F32 = jnp.float32
BF16 = jnp.bfloat16
ROOT = math.sqrt(3.0) / 2.0


def split(value):
    high = value.astype(BF16)
    return high, (value - high.astype(F32)).astype(BF16)


def dot(left, right, form=((1,), (0,))):
    return lax.dot_general(left, right, (form, ((), ())), preferred_element_type=F32)


def dot_left(table_high, table_low, value, form=((1,), (0,))):
    high, low = split(value)
    return dot(table_high, high, form) + (dot(table_high, low, form) + dot(table_low, high, form))


def dot_right(value, table_high, table_low):
    high, low = split(value)
    return dot(high, table_high) + (dot(low, table_high) + dot(high, table_low))


def butterfly(parts, sign):
    (a_r, a_i), (b_r, b_i), (c_r, c_i) = parts
    sum_r, sum_i = b_r + c_r, b_i + c_i
    dif_r, dif_i = (sign * ROOT) * (b_r - c_r), (sign * ROOT) * (b_i - c_i)
    mid_r, mid_i = a_r - 0.5 * sum_r, a_i - 0.5 * sum_i
    return (
        (a_r + sum_r, a_i + sum_i),
        (mid_r - dif_i, mid_i + dif_r),
        (mid_r + dif_i, mid_i - dif_r),
    )


def dft_tables(length):
    base = length // RADIX
    index = np.arange(base)
    whole = np.arange(length)
    angle = (index[:, None] * whole[None, :] % length) * (2.0 * np.pi / length)
    real = np.cos(angle) / np.sqrt(length)
    imag = -np.sin(angle) / np.sqrt(length)
    tables = []
    for part in range(RADIX):
        re, im = real[:, part::RADIX], imag[:, part::RADIX]
        right = np.block([[re, im], [-im, re]])
        left = np.block([[re, -im], [im, re]])
        tables.append((left, left.T, right, right.T))
    full = np.array(tables, dtype=np.float32)
    high = full.astype(ml_dtypes.bfloat16)
    low = (full - high.astype(np.float32)).astype(ml_dtypes.bfloat16)
    return np.stack((high, low), 2)


def mark_blocks(column_ref, marks):
    step = 256
    tiles = column_ref.shape[1]

    def fill(chunk, carry):
        start = pl.multiple_of(chunk * step, step)
        rows = lax.broadcasted_iota(jnp.int32, (step, tiles), 0) + start
        marks[pl.ds(start, step), :] = (rows == column_ref[...]).astype(F32).astype(BF16)
        return carry

    lax.fori_loop(0, marks.shape[0] // step, fill, 0)


def add_blocks(back_high, back_low, marks, grid):
    step = 768

    def chunk(index, carry):
        start = pl.multiple_of(index * step, step)
        mark = marks[pl.ds(start, step), :]
        rows = ((1,), (1,))
        grid[:, pl.ds(start, step)] = dot(back_high[...], mark, rows) + dot(back_low[...], mark, rows)
        return carry

    lax.fori_loop(0, marks.shape[0] // step, chunk, 0)


def grid_to_image(grid, tables, middle, maps, out):
    xpos, _, base, length = maps.shape[1:]
    span = xpos * length
    for x in range(xpos):
        lanes = slice(x * length, (x + 1) * length)
        parts = []
        for q in range(RADIX):
            part = grid[:, q * span + x * length : q * span + (x + 1) * length]
            parts.append((part[:base], part[base:]))
        for b, (re, im) in enumerate(butterfly(parts, 1.0)):
            value = jnp.concatenate((re, im), 0)
            middle[b, :, lanes] = dot_left(tables[b, 1, 0], tables[b, 1, 1], value)

    def rows(index, carry):
        x, b = index // RADIX, index % RADIX
        parts = []
        for r in range(RADIX):
            start = pl.multiple_of(x * length + r * base, base)
            value = middle[b, :, pl.ds(start, base)]
            value = jnp.concatenate((value[:base], value[base:]), 1)
            back = dot_right(value, tables[r, 3, 0], tables[r, 3, 1])
            parts.append((back[:, :base], back[:, base:]))
        for q, (re, im) in enumerate(butterfly(parts, 1.0)):
            lanes = slice(q * base, (q + 1) * base)
            map_r, map_i = maps[0, x, b, :, lanes], maps[1, x, b, :, lanes]
            out[0, x, b, :, lanes] = map_r * re + map_i * im
            out[1, x, b, :, lanes] = map_r * im - map_i * re
        return carry

    lax.fori_loop(0, xpos * RADIX, rows, 0)


def image_to_grid(image, tables, middle, maps, grid_high, grid_low):
    xpos, _, base, length = maps.shape[1:]
    span = xpos * length

    def rows(index, carry):
        x, b = index // RADIX, index % RADIX
        parts = []
        for q in range(RADIX):
            lanes = slice(q * base, (q + 1) * base)
            map_r, map_i = maps[0, x, b, :, lanes], maps[1, x, b, :, lanes]
            re, im = image[0, x, b, :, lanes], image[1, x, b, :, lanes]
            parts.append((map_r * re - map_i * im, map_r * im + map_i * re))
        for r, (re, im) in enumerate(butterfly(parts, -1.0)):
            value = dot_right(jnp.concatenate((re, im), 1), tables[r, 2, 0], tables[r, 2, 1])
            start = pl.multiple_of(x * length + r * base, base)
            middle[b, :base, pl.ds(start, base)] = value[:, :base]
            middle[b, base:, pl.ds(start, base)] = value[:, base:]
        return carry

    lax.fori_loop(0, xpos * RADIX, rows, 0)
    for x in range(xpos):
        parts = []
        for b in range(RADIX):
            value = middle[b, :, x * length : (x + 1) * length]
            value = dot_left(tables[b, 0, 0], tables[b, 0, 1], value)
            parts.append((value[:base], value[base:]))
        for q, (re, im) in enumerate(butterfly(parts, -1.0)):
            high, low = split(jnp.concatenate((re, im), 0))
            lanes = slice(q * span + x * length, q * span + (x + 1) * length)
            grid_high[:, lanes] = high
            grid_low[:, lanes] = low


def rhs_kernel(samples, weight, kernel, column, tables, maps, out, marks, back_high, back_low, middle, grid):
    base = kernel.shape[0]
    mark_blocks(column, marks)
    kernel_t = kernel[...].T
    kernel_high, kernel_low = split(kernel_t)
    for part in range(2):
        value = samples[part] * weight[...]
        back = dot_left(kernel_high, kernel_low, value, ((1,), (1,)))
        high, low = split(back)
        back_high[part * base : (part + 1) * base, :] = high
        back_low[part * base : (part + 1) * base, :] = low
    add_blocks(back_high, back_low, marks, grid)
    grid_to_image(grid, tables, middle, maps, out)


def normal_kernel(image, weight, kernel, column, tables, maps, out, marks, back_high, back_low, middle, grid, grid_high, grid_low):
    base = kernel.shape[0]
    mark_blocks(column, marks)
    image_to_grid(image, tables, middle, maps, grid_high, grid_low)
    kernel_high, kernel_low = split(kernel[...])
    turned_high, turned_low = split(kernel[...].T)
    step = 256

    def sample(index, carry):
        start = pl.multiple_of(index * step, step)
        mark = marks[:, pl.ds(start, step)]
        picked = dot(grid_high[...], mark) + dot(grid_low[...], mark)
        for part in range(2):
            rows = slice(part * base, (part + 1) * base)
            value = dot_left(kernel_high, kernel_low, picked[rows]) * weight[:, pl.ds(start, step)]
            high, low = split(dot_left(turned_high, turned_low, value))
            back_high[rows, pl.ds(start, step)] = high
            back_low[rows, pl.ds(start, step)] = low
        return carry

    lax.fori_loop(0, marks.shape[1] // step, sample, 0)
    add_blocks(back_high, back_low, marks, grid)
    grid_to_image(grid, tables, middle, maps, out)


def call(kernel, image_shape, tiles, forward):
    base, length = image_shape[-2:]
    cells = image_shape[1] * RADIX * length
    scratch = [
        pltpu.VMEM((cells, tiles), BF16),
        pltpu.VMEM((2 * base, tiles), BF16),
        pltpu.VMEM((2 * base, tiles), BF16),
        pltpu.VMEM((RADIX, 2 * base, image_shape[1] * length), F32),
        pltpu.VMEM((2 * base, cells), F32),
    ]
    if forward:
        scratch += [pltpu.VMEM((2 * base, cells), BF16)] * 2
    return pl.pallas_call(
        kernel,
        out_shape=jax.ShapeDtypeStruct(image_shape, F32),
        in_specs=[pl.BlockSpec(memory_space=pltpu.VMEM)] * 6,
        out_specs=pl.BlockSpec(memory_space=pltpu.VMEM),
        scratch_shapes=scratch,
        compiler_params=pltpu.CompilerParams(vmem_limit_bytes=56 * 2**20),
    )


def whole_coils(coil_maps, samples, kernel, tile_block, tile_count, dcf_level, dcf_table):
    ncoil, _, xpos, zdev, ylen = coil_maps.shape
    base = kernel.shape[0]
    slabs = lax.axis_size("slab")
    slab = lax.axis_index("slab")
    ky_dev = ylen // slabs
    lines = zdev // RADIX
    zblocks = zdev * slabs // base

    near = coil_maps.reshape(ncoil, 2, xpos, lines, RADIX, ylen).transpose(0, 1, 2, 4, 3, 5)
    maps = lax.all_to_all(near, "slab", split_axis=0, concat_axis=4, tiled=True)[0]
    data = lax.all_to_all(samples, "slab", split_axis=0, concat_axis=2, tiled=True)[0]

    cells = jnp.stack((tile_block, tile_count, dcf_level))
    cells = lax.all_gather(cells, "slab", axis=1, tiled=True)
    block, count, level = cells[0], cells[1], cells[2]
    tiles = block.shape[0]
    shard = jnp.arange(tiles, dtype=jnp.int32) // (tiles // slabs)
    ky = shard * ky_dev + block // zblocks % ky_dev
    column = (block % zblocks * xpos + block // (zblocks * ky_dev)) * ylen
    column = (column + ky % RADIX * base + ky // RADIX)[None, :]
    levels = jnp.arange(dcf_table.shape[0], dtype=jnp.int32)
    density = jnp.sum(jnp.where(level[:, None] == levels[None, :], dcf_table[None, :], 0.0), axis=1)
    position = jnp.arange(base, dtype=jnp.int32)
    weight = jnp.where(position[None, :] < count[:, None], density[:, None], 0.0)
    weight_t = jnp.where(position[:, None] < count[None, :], density[None, :], 0.0)

    tables = jnp.asarray(dft_tables(ylen))
    shape = maps.shape

    def total(local):
        return lax.psum(local, ("slab", "coil"))

    rhs = total(call(rhs_kernel, shape, tiles, False)(data, weight, kernel, column, tables, maps))
    solution = jnp.zeros_like(rhs)
    residual = rhs
    direction = rhs
    norm_now = jnp.sum(residual * residual)
    normal = call(normal_kernel, shape, tiles, True)
    for step in range(ITERS):
        image = total(normal(direction, weight_t, kernel, column, tables, maps)) + SHIFT * direction
        alpha = norm_now / jnp.sum(direction * image)
        solution = solution + alpha * direction
        residual = residual - alpha * image
        norm_next = jnp.sum(residual * residual)
        direction = residual + norm_next / norm_now * direction
        norm_now = norm_next

    def own(value):
        piece = lax.dynamic_slice_in_dim(value, slab * lines, lines, 3)
        return piece.transpose(0, 1, 3, 2, 4).reshape(2, xpos, zdev, ylen)

    return own(solution), own(residual)


def fits(mesh, coil_maps, samples, kernel):
    slabs, coils = mesh.shape["slab"], mesh.shape["coil"]
    coil_dev = coil_maps.shape[0] // coils
    zlen, ylen = coil_maps.shape[3:]
    base = kernel.shape[0]
    return (
        coil_dev == slabs
        and zlen == ylen == RADIX * base
        and base == 128
        and zlen % (slabs * RADIX) == 0
        and samples.shape[2] % 256 == 0
    )


def solution(mesh):
    placed = (
        P("coil", "scan", None, "slab", None),
        P("coil", "scan", "slab", None),
        P(),
        P("slab"),
        P("slab"),
        P("slab"),
        P(),
    )

    def run(coil_maps, samples, kernel, *rest):
        chosen = whole_coils if fits(mesh, coil_maps, samples, kernel) else body
        return jax.shard_map(
            chosen,
            mesh=mesh,
            in_specs=placed,
            out_specs=(P("scan", None, "slab", None), P("scan", None, "slab", None)),
            check_vma=False,
        )(coil_maps, samples, kernel, *rest)

    return run
```

```python
import math

import jax
import jax.numpy as jnp
import ml_dtypes
import numpy as np
from jax import lax
from jax.experimental import pallas as pl
from jax.experimental.pallas import tpu as pltpu
from jax.sharding import PartitionSpec as P

ITERS = 2


HIGH = lax.Precision.HIGHEST
SHIFT = 0.5


def tables(count):
    index = jnp.arange(count, dtype=jnp.int32)
    phase = index[:, None] * index[None, :] % count
    angle = phase.astype(jnp.float32) * (2.0 * math.pi / count)
    factor = 1.0 / math.sqrt(count)
    return (jnp.cos(angle) * factor, jnp.sin(angle) * factor)


def transform(real, imag, cosine, sine, sign, form):
    rc = jnp.einsum(form, real, cosine, precision=HIGH)
    rs = jnp.einsum(form, real, sine, precision=HIGH)
    mc = jnp.einsum(form, imag, cosine, precision=HIGH)
    ms = jnp.einsum(form, imag, sine, precision=HIGH)
    return (rc - sign * ms, mc + sign * rs)


def body(coil_maps, samples, kernel, tile_block, tile_count, dcf_level, dcf_table):
    ncoil, _, xpos, zdev, ylen = coil_maps.shape
    blocklen = kernel.shape[0]
    slabs = lax.axis_size("slab")
    zlen = zdev * slabs
    ky_dev = ylen // slabs
    nblocks = xpos * ky_dev * (zlen // blocklen)
    cos_y, sin_y = tables(ylen)
    cos_z, sin_z = tables(zlen)
    levels = jnp.arange(dcf_table.shape[0], dtype=jnp.int32)
    density = jnp.sum(
        jnp.where(dcf_level[:, None] == levels[None, :], dcf_table[None, :], 0.0), axis=1
    )
    valid = (jnp.arange(blocklen, dtype=jnp.int32)[None, :] < tile_count[:, None]).astype(
        jnp.float32
    )
    weight = density[:, None] * valid
    map_r = coil_maps[:, 0]
    map_i = coil_maps[:, 1]

    def inverse_y(piece):
        out_r, out_i = transform(piece[:, 0], piece[:, 1], cos_y, sin_y, 1.0, "cxzn,nk->cxzk")
        return jnp.stack((out_r, out_i), 1)

    def to_image(values):
        back = jnp.einsum("cita,ab->citb", values, kernel, precision=HIGH)
        blank = jnp.zeros((ncoil, 2, nblocks, blocklen), jnp.float32)
        grid = blank.at[:, :, tile_block].add(back).reshape(ncoil, 2, xpos, ky_dev, zlen)
        part_r, part_i = transform(grid[:, 0], grid[:, 1], cos_z, sin_z, 1.0, "cxyk,zk->cxzy")
        spectra = jnp.stack((part_r, part_i), 1)
        coils = inverse_y(lax.all_to_all(spectra, "slab", split_axis=3, concat_axis=4, tiled=True))
        coil_r = coils[:, 0]
        coil_i = coils[:, 1]
        sum_r = jnp.sum(map_r * coil_r + map_i * coil_i, axis=0)
        sum_i = jnp.sum(map_r * coil_i - map_i * coil_r, axis=0)
        return jnp.stack((sum_r, sum_i), 0)

    rhs_local = to_image(samples * weight)

    def total(local):
        return lax.psum(local, "coil")

    def inner(first, second):
        return lax.psum(jnp.sum(first * second), "slab")

    rhs = total(rhs_local)
    solution = jnp.zeros_like(rhs)
    residual = rhs
    direction = rhs
    norm_now = inner(residual, residual)
    for step in range(ITERS):
        sample_coil_r = map_r * direction[0][None] - map_i * direction[1][None]
        sample_coil_i = map_r * direction[1][None] + map_i * direction[0][None]
        spec_r, spec_i = transform(
            sample_coil_r, sample_coil_i, cos_y, sin_y, -1.0, "cxzn,nk->cxzk"
        )
        sample_spectra = jnp.stack((spec_r, spec_i), 1)
        forward_piece = lax.all_to_all(
            sample_spectra, "slab", split_axis=4, concat_axis=3, tiled=True
        )
        forward_out_r, forward_out_i = transform(
            forward_piece[:, 0], forward_piece[:, 1], cos_z, sin_z, -1.0, "cxzy,zk->cxyk"
        )
        sample_grid = jnp.stack((forward_out_r, forward_out_i), 1)
        blocks = sample_grid.reshape(ncoil, 2, nblocks, blocklen)
        picked = blocks[:, :, tile_block]
        image = (
            total(to_image(jnp.einsum("citb,ab->cita", picked, kernel, precision=HIGH) * weight))
            + SHIFT * direction
        )
        alpha = norm_now / inner(direction, image)
        solution = solution + alpha * direction
        residual = residual - alpha * image
        norm_next = inner(residual, residual)
        direction = residual + norm_next / norm_now * direction
        norm_now = norm_next
    return (solution, residual)


RADIX = 3
F32 = jnp.float32
BF16 = jnp.bfloat16
ROOT = math.sqrt(3.0) / 2.0


def split(value):
    high = value.astype(BF16)
    return high, (value - high.astype(F32)).astype(BF16)


def dot(left, right, form=((1,), (0,))):
    return lax.dot_general(left, right, (form, ((), ())), preferred_element_type=F32)


def dot_left(table_high, table_low, value, form=((1,), (0,))):
    high, low = split(value)
    return dot(table_high, high, form) + (dot(table_high, low, form) + dot(table_low, high, form))


def dot_right(value, table_high, table_low):
    high, low = split(value)
    return dot(high, table_high) + (dot(low, table_high) + dot(high, table_low))


def butterfly(parts, sign):
    (a_r, a_i), (b_r, b_i), (c_r, c_i) = parts
    sum_r, sum_i = b_r + c_r, b_i + c_i
    dif_r, dif_i = (sign * ROOT) * (b_r - c_r), (sign * ROOT) * (b_i - c_i)
    mid_r, mid_i = a_r - 0.5 * sum_r, a_i - 0.5 * sum_i
    return (
        (a_r + sum_r, a_i + sum_i),
        (mid_r - dif_i, mid_i + dif_r),
        (mid_r + dif_i, mid_i - dif_r),
    )


def dft_tables(length):
    base = length // RADIX
    index = np.arange(base)
    whole = np.arange(length)
    angle = (index[:, None] * whole[None, :] % length) * (2.0 * np.pi / length)
    real = np.cos(angle) / np.sqrt(length)
    imag = -np.sin(angle) / np.sqrt(length)
    tables = []
    for part in range(RADIX):
        re, im = real[:, part::RADIX], imag[:, part::RADIX]
        right = np.block([[re, im], [-im, re]])
        left = np.block([[re, -im], [im, re]])
        tables.append((left, left.T, right, right.T))
    full = np.array(tables, dtype=np.float32)
    high = full.astype(ml_dtypes.bfloat16)
    low = (full - high.astype(np.float32)).astype(ml_dtypes.bfloat16)
    return np.stack((high, low), 2)


def mark_blocks(column_ref, marks):
    step = 128
    tiles = column_ref.shape[1]

    def fill(chunk, carry):
        start = pl.multiple_of(chunk * step, step)
        rows = lax.broadcasted_iota(jnp.int32, (step, tiles), 0) + start
        marks[pl.ds(start, step), :] = (rows == column_ref[...]).astype(F32).astype(BF16)
        return carry

    lax.fori_loop(0, marks.shape[0] // step, fill, 0)


def add_blocks(back_high, back_low, marks, grid):
    step = 384

    def chunk(index, carry):
        start = pl.multiple_of(index * step, step)
        mark = marks[pl.ds(start, step), :]
        rows = ((1,), (1,))
        grid[:, pl.ds(start, step)] = dot(back_high[...], mark, rows) + dot(back_low[...], mark, rows)
        return carry

    lax.fori_loop(0, marks.shape[0] // step, chunk, 0)


def grid_to_image(grid, tables, middle, maps, out):
    coils, _, _, base, length = maps.shape
    for c in range(coils):
        parts = []
        for q in range(RADIX):
            part = grid[2 * base * c : 2 * base * (c + 1), q * length : (q + 1) * length]
            parts.append((part[:base], part[base:]))
        for b, (re, im) in enumerate(butterfly(parts, 1.0)):
            value = jnp.concatenate((re, im), 0)
            middle[b, :, c * length : (c + 1) * length] = dot_left(tables[b, 1, 0], tables[b, 1, 1], value)

    def rows(b, carry):
        sums = [None] * RADIX
        for c in range(coils):
            parts = []
            for r in range(RADIX):
                start = c * length + r * base
                value = middle[b, :, start : start + base]
                value = jnp.concatenate((value[:base], value[base:]), 1)
                back = dot_right(value, tables[r, 3, 0], tables[r, 3, 1])
                parts.append((back[:, :base], back[:, base:]))
            for q, (re, im) in enumerate(butterfly(parts, 1.0)):
                lanes = slice(q * base, (q + 1) * base)
                map_r, map_i = maps[c, 0, b, :, lanes], maps[c, 1, b, :, lanes]
                term = (map_r * re + map_i * im, map_r * im - map_i * re)
                if c:
                    term = (sums[q][0] + term[0], sums[q][1] + term[1])
                sums[q] = term
        for q in range(RADIX):
            lanes = slice(q * base, (q + 1) * base)
            out[0, b, :, lanes], out[1, b, :, lanes] = sums[q]
        return carry

    lax.fori_loop(0, RADIX, rows, 0)


def image_to_grid(image, tables, middle, maps, grid_high, grid_low):
    coils, _, _, base, length = maps.shape

    def rows(b, carry):
        for c in range(coils):
            parts = []
            for q in range(RADIX):
                lanes = slice(q * base, (q + 1) * base)
                map_r, map_i = maps[c, 0, b, :, lanes], maps[c, 1, b, :, lanes]
                re, im = image[0, b, :, lanes], image[1, b, :, lanes]
                parts.append((map_r * re - map_i * im, map_r * im + map_i * re))
            for r, (re, im) in enumerate(butterfly(parts, -1.0)):
                value = dot_right(jnp.concatenate((re, im), 1), tables[r, 2, 0], tables[r, 2, 1])
                start = c * length + r * base
                middle[b, :base, start : start + base] = value[:, :base]
                middle[b, base:, start : start + base] = value[:, base:]
        return carry

    lax.fori_loop(0, RADIX, rows, 0)
    for c in range(coils):
        parts = []
        for b in range(RADIX):
            value = middle[b, :, c * length : (c + 1) * length]
            value = dot_left(tables[b, 0, 0], tables[b, 0, 1], value)
            parts.append((value[:base], value[base:]))
        for q, (re, im) in enumerate(butterfly(parts, -1.0)):
            high, low = split(jnp.concatenate((re, im), 0))
            rows_c, lanes = slice(2 * base * c, 2 * base * (c + 1)), slice(q * length, (q + 1) * length)
            grid_high[rows_c, lanes] = high
            grid_low[rows_c, lanes] = low


def rhs_kernel(samples, weight, kernel, column, tables, maps, out, marks, back_high, back_low, middle, grid):
    base = kernel.shape[0]
    mark_blocks(column, marks)
    kernel_high, kernel_low = split(kernel[...].T)
    for part in range(samples.shape[0]):
        value = samples[part] * weight[...]
        back = dot_left(kernel_high, kernel_low, value, ((1,), (1,)))
        high, low = split(back)
        back_high[part * base : (part + 1) * base, :] = high
        back_low[part * base : (part + 1) * base, :] = low
    add_blocks(back_high, back_low, marks, grid)
    grid_to_image(grid, tables, middle, maps, out)


def normal_kernel(image, weight, kernel, column, tables, maps, out, marks, back_high, back_low, middle, grid, grid_high, grid_low):
    base = kernel.shape[0]
    mark_blocks(column, marks)
    image_to_grid(image, tables, middle, maps, grid_high, grid_low)
    kernel_high, kernel_low = split(kernel[...])
    turned_high, turned_low = split(kernel[...].T)
    step = 256

    def sample(index, carry):
        start = pl.multiple_of(index * step, step)
        mark = marks[:, pl.ds(start, step)]
        picked = dot(grid_high[...], mark) + dot(grid_low[...], mark)
        for part in range(picked.shape[0] // base):
            rows = slice(part * base, (part + 1) * base)
            value = dot_left(kernel_high, kernel_low, picked[rows]) * weight[:, pl.ds(start, step)]
            high, low = split(dot_left(turned_high, turned_low, value))
            back_high[rows, pl.ds(start, step)] = high
            back_low[rows, pl.ds(start, step)] = low
        return carry

    lax.fori_loop(0, marks.shape[1] // step, sample, 0)
    add_blocks(back_high, back_low, marks, grid)
    grid_to_image(grid, tables, middle, maps, out)


def call(kernel, map_shape, tiles, forward):
    coils, _, _, base, length = map_shape
    cells = RADIX * length
    rows = 2 * base * coils
    scratch = [
        pltpu.VMEM((cells, tiles), BF16),
        pltpu.VMEM((rows, tiles), BF16),
        pltpu.VMEM((rows, tiles), BF16),
        pltpu.VMEM((RADIX, 2 * base, coils * length), F32),
        pltpu.VMEM((rows, cells), F32),
    ]
    if forward:
        scratch += [pltpu.VMEM((rows, cells), BF16)] * 2
    return pl.pallas_call(
        kernel,
        out_shape=jax.ShapeDtypeStruct(map_shape[1:], F32),
        in_specs=[pl.BlockSpec(memory_space=pltpu.VMEM)] * 6,
        out_specs=pl.BlockSpec(memory_space=pltpu.VMEM),
        scratch_shapes=scratch,
        compiler_params=pltpu.CompilerParams(vmem_limit_bytes=56 * 2**20),
    )


CHUNKS = 4
STEP = 96


def combine(first, refs):
    if first:
        part, direction_out, norm_out, whole, landed, work, tile, send, recv = refs
    else:
        (part, direction, residual, answer, norm, direction_out, residual_out, answer_out, norm_out,
         whole, landed, work, tile, send, recv) = refs
    slab, coil = lax.axis_index("slab"), lax.axis_index("coil")
    core, chip, far, near = coil % 2, coil // 2, slab // 2, slab % 2
    partners = (
        {"coil": chip * 2 + (1 - core)},
        {"coil": (1 - chip) * 2 + core},
        {"slab": (1 - far) * 2 + near},
        {"slab": far * 2 + (1 - near)},
    )
    bits = (core, chip, far)
    barrier = pltpu.get_barrier_semaphore()
    for partner in partners:
        pl.semaphore_signal(barrier, inc=1, device_id=partner, device_id_type=pl.DeviceIdType.MESH)
    pl.semaphore_wait(barrier, len(partners))

    total = part.shape[0]
    size = total // CHUNKS
    sent = []

    def rows(start, count):
        return pl.ds(pl.multiple_of(start, 8), count)

    def push(source, target, slot, axis):
        copy = pltpu.make_async_remote_copy(
            src_ref=source,
            dst_ref=target,
            send_sem=send.at[slot],
            recv_sem=recv.at[slot],
            device_id=partners[axis],
            device_id_type=pl.DeviceIdType.MESH,
        )
        copy.start()
        sent.append(copy)
        return copy

    orders = [(0, 1, 2) if chunk % 2 == 0 else (0, 2, 1) for chunk in range(CHUNKS)]
    starts = [chunk * size for chunk in range(CHUNKS)]
    flying = [None] * CHUNKS
    place = [0, size // 2, size // 2 + size // 4]
    slots = [[None] * 3 for _ in range(CHUNKS)]
    for stage in range(4):
        for chunk in range(CHUNKS):
            count = size >> stage
            if stage:
                flying[chunk].wait_recv()
                mine = rows(starts[chunk], count)
                arrived = landed[chunk, place[stage - 1] : place[stage - 1] + count, :]
                held = part if stage == 1 else work
                goal = whole if stage == 3 else work
                goal[mine, :] = held[mine, :] + arrived
            if stage < 3:
                half = count // 2
                bit = bits[orders[chunk][stage]]
                other = starts[chunk] + (1 - bit) * half
                source = part if stage == 0 else work
                target = landed.at[chunk, pl.ds(place[stage], half), :]
                flying[chunk] = push(source.at[rows(other, half), :], target, chunk * 6 + stage, orders[chunk][stage])
                starts[chunk] = starts[chunk] + bit * half
    for stage in range(4):
        for chunk in range(CHUNKS):
            if stage:
                flying[chunk].wait_recv()
                axis = orders[chunk][3 - stage]
                starts[chunk] = starts[chunk] - bits[axis] * (size >> (4 - stage))
            if stage < 3:
                axis = orders[chunk][2 - stage]
                mine = whole.at[rows(starts[chunk], size >> (3 - stage)), :]
                flying[chunk] = push(mine, mine, chunk * 6 + 3 + stage, axis)

    for copy in sent:
        copy.wait_send()
    sent.clear()

    def exchange(value, index):
        tile[index, 0] = jnp.broadcast_to(value, tile.shape[2:])
        copy = push(tile.at[index, 0], tile.at[index, 1], CHUNKS * 6 + index, 3)
        copy.wait_recv()
        return (tile[index, 0] + tile[index, 1])[:1, :1]

    def sweep(body):
        def step(index, carry):
            return carry + body(rows(index * STEP, STEP))

        lanes = lax.fori_loop(0, total // STEP, step, jnp.zeros((8, part.shape[1]), F32))
        return jnp.sum(lanes, keepdims=True)

    def fold(value):
        return jnp.sum(value.reshape(-1, 8, value.shape[1]), 0)

    if first:

        def copy_out(at):
            value = whole[at, :]
            direction_out[at, :] = value
            return fold(value * value)

        norm_out[...] = jnp.broadcast_to(exchange(sweep(copy_out), 0), norm_out.shape)
    else:

        def meet(at):
            move = direction[at, :]
            image = whole[at, :] + SHIFT * move
            work[at, :] = image
            return fold(move * image)

        before = norm[:1, :1]
        alpha = before / exchange(sweep(meet), 0)

        def shrink(at):
            left = residual[at, :] - alpha * work[at, :]
            residual_out[at, :] = left
            answer_out[at, :] = answer[at, :] + alpha * direction[at, :]
            return fold(left * left)

        after = exchange(sweep(shrink), 1)
        beta = after / before

        def turn(index, carry):
            at = rows(index * STEP, STEP)
            direction_out[at, :] = residual_out[at, :] + beta * direction[at, :]
            return carry

        lax.fori_loop(0, total // STEP, turn, 0)
        norm_out[...] = jnp.broadcast_to(after, norm_out.shape)
    for copy in sent:
        copy.wait_send()


def first_kernel(*refs):
    combine(True, refs)


def next_kernel(*refs):
    combine(False, refs)


def combine_call(first, shape):
    image = jax.ShapeDtypeStruct(shape, F32)
    scalar = jax.ShapeDtypeStruct((8, 128), F32)
    copies = CHUNKS * 6 + 2
    memory = pl.BlockSpec(memory_space=pltpu.VMEM)
    return pl.pallas_call(
        first_kernel if first else next_kernel,
        out_shape=(image, scalar) if first else (image, image, image, scalar),
        in_specs=[memory] * (1 if first else 5),
        out_specs=[memory] * (2 if first else 4),
        scratch_shapes=[
            pltpu.VMEM(shape, F32),
            pltpu.VMEM((CHUNKS, shape[0] // CHUNKS, shape[1]), F32),
            pltpu.VMEM(shape, F32),
            pltpu.VMEM((2, 2, 8, 128), F32),
            pltpu.SemaphoreType.DMA((copies,)),
            pltpu.SemaphoreType.DMA((copies,)),
        ],
        compiler_params=pltpu.CompilerParams(
            collective_id=0 if first else 1, has_side_effects=True, vmem_limit_bytes=56 * 2**20
        ),
    )


def whole_coils(coil_maps, samples, kernel, tile_block, tile_count, dcf_level, dcf_table):
    ncoil, _, xpos, zdev, ylen = coil_maps.shape
    base = kernel.shape[0]
    slabs = lax.axis_size("slab")
    slab = lax.axis_index("slab")
    ky_dev = ylen // slabs
    lines = zdev // RADIX
    zblocks = zdev * slabs // base
    pairs = slabs // xpos
    group = ncoil // pairs

    near = coil_maps.reshape(pairs, group, 2, xpos, lines, RADIX, ylen).transpose(0, 3, 1, 2, 5, 4, 6)
    near = near.reshape(slabs, group, 2, RADIX, lines, ylen)
    data = samples.reshape(pairs, 1, group * 2, *samples.shape[2:])
    data = jnp.broadcast_to(data, (pairs, xpos, *data.shape[2:])).reshape(slabs, *data.shape[2:])
    data = lax.all_to_all(data, "slab", split_axis=0, concat_axis=2, tiled=True)[0]
    maps = lax.all_to_all(near, "slab", split_axis=0, concat_axis=4, tiled=True)[0]

    cells = jnp.stack((tile_block, tile_count, dcf_level))
    cells = lax.all_gather(cells, "slab", axis=1, tiled=True)
    block, count, level = cells[0], cells[1], cells[2]
    tiles = block.shape[0]
    shard = jnp.arange(tiles, dtype=jnp.int32) // (tiles // slabs)
    ky = shard * ky_dev + block // zblocks % ky_dev
    column = block % zblocks * ylen + ky % RADIX * base + ky // RADIX
    column = jnp.where(block // (zblocks * ky_dev) == slab % xpos, column, -1)[None, :]
    levels = jnp.arange(dcf_table.shape[0], dtype=jnp.int32)
    density = jnp.sum(jnp.where(level[:, None] == levels[None, :], dcf_table[None, :], 0.0), axis=1)
    position = jnp.arange(base, dtype=jnp.int32)
    weight = jnp.where(position[None, :] < count[:, None], density[:, None], 0.0)
    weight_t = jnp.where(position[:, None] < count[None, :], density[None, :], 0.0)

    tables = jnp.asarray(dft_tables(ylen))
    shape = maps.shape
    flat = (2 * RADIX * base, ylen)

    partial = call(rhs_kernel, shape, tiles, False)(data, weight, kernel, column, tables, maps)
    direction, norm = combine_call(True, flat)(partial.reshape(flat))
    residual, answer = direction, jnp.zeros_like(direction)
    normal = call(normal_kernel, shape, tiles, True)
    update = combine_call(False, flat)
    for step in range(ITERS):
        partial = normal(direction.reshape(shape[1:]), weight_t, kernel, column, tables, maps)
        direction, residual, answer, norm = update(partial.reshape(flat), direction, residual, answer, norm)

    both = jnp.stack((answer, residual)).reshape(2, 2, RADIX, base, ylen)
    partner = slab + 1 - 2 * (slab % 2)
    keep = lax.dynamic_slice_in_dim(both, slab * lines, lines, 3)
    give = lax.dynamic_slice_in_dim(both, partner * lines, lines, 3)
    take = lax.ppermute(give, "slab", [(index, index ^ 1) for index in range(slabs)])
    low = slab % 2 == 0
    both = jnp.stack((jnp.where(low, keep, take), jnp.where(low, take, keep)), 2)
    both = both.transpose(0, 1, 2, 4, 3, 5).reshape(2, 2, xpos, zdev, ylen)
    return both[0], both[1]


def fits(mesh, coil_maps, samples, kernel):
    slabs, coils = mesh.shape["slab"], mesh.shape["coil"]
    coil_dev = coil_maps.shape[0] // coils
    zlen, ylen = coil_maps.shape[3:]
    base = kernel.shape[0]
    return (
        coil_dev == slabs == coils == 4
        and coil_maps.shape[2] == 2
        and zlen == ylen == RADIX * base
        and base == 128
        and zlen % (slabs * RADIX) == 0
        and samples.shape[2] % 256 == 0
    )


def solution(mesh):
    placed = (
        P("coil", "scan", None, "slab", None),
        P("coil", "scan", "slab", None),
        P(),
        P("slab"),
        P("slab"),
        P("slab"),
        P(),
    )

    def run(coil_maps, samples, kernel, *rest):
        chosen = whole_coils if fits(mesh, coil_maps, samples, kernel) else body
        return jax.shard_map(
            chosen,
            mesh=mesh,
            in_specs=placed,
            out_specs=(P("scan", None, "slab", None), P("scan", None, "slab", None)),
            check_vma=False,
        )(coil_maps, samples, kernel, *rest)

    return run
```

```python
import math

import jax
import jax.numpy as jnp
import ml_dtypes
import numpy as np
from jax import lax
from jax.experimental import pallas as pl
from jax.experimental.pallas import tpu as pltpu
from jax.sharding import PartitionSpec as P

ITERS = 2


HIGH = lax.Precision.HIGHEST
SHIFT = 0.5


def tables(count):
    index = jnp.arange(count, dtype=jnp.int32)
    phase = index[:, None] * index[None, :] % count
    angle = phase.astype(jnp.float32) * (2.0 * math.pi / count)
    factor = 1.0 / math.sqrt(count)
    return (jnp.cos(angle) * factor, jnp.sin(angle) * factor)


def transform(real, imag, cosine, sine, sign, form):
    rc = jnp.einsum(form, real, cosine, precision=HIGH)
    rs = jnp.einsum(form, real, sine, precision=HIGH)
    mc = jnp.einsum(form, imag, cosine, precision=HIGH)
    ms = jnp.einsum(form, imag, sine, precision=HIGH)
    return (rc - sign * ms, mc + sign * rs)


def body(coil_maps, samples, kernel, tile_block, tile_count, dcf_level, dcf_table):
    ncoil, _, xpos, zdev, ylen = coil_maps.shape
    blocklen = kernel.shape[0]
    slabs = lax.axis_size("slab")
    zlen = zdev * slabs
    ky_dev = ylen // slabs
    nblocks = xpos * ky_dev * (zlen // blocklen)
    cos_y, sin_y = tables(ylen)
    cos_z, sin_z = tables(zlen)
    levels = jnp.arange(dcf_table.shape[0], dtype=jnp.int32)
    density = jnp.sum(
        jnp.where(dcf_level[:, None] == levels[None, :], dcf_table[None, :], 0.0), axis=1
    )
    valid = (jnp.arange(blocklen, dtype=jnp.int32)[None, :] < tile_count[:, None]).astype(
        jnp.float32
    )
    weight = density[:, None] * valid
    map_r = coil_maps[:, 0]
    map_i = coil_maps[:, 1]

    def inverse_y(piece):
        out_r, out_i = transform(piece[:, 0], piece[:, 1], cos_y, sin_y, 1.0, "cxzn,nk->cxzk")
        return jnp.stack((out_r, out_i), 1)

    def to_image(values):
        back = jnp.einsum("cita,ab->citb", values, kernel, precision=HIGH)
        blank = jnp.zeros((ncoil, 2, nblocks, blocklen), jnp.float32)
        grid = blank.at[:, :, tile_block].add(back).reshape(ncoil, 2, xpos, ky_dev, zlen)
        part_r, part_i = transform(grid[:, 0], grid[:, 1], cos_z, sin_z, 1.0, "cxyk,zk->cxzy")
        spectra = jnp.stack((part_r, part_i), 1)
        coils = inverse_y(lax.all_to_all(spectra, "slab", split_axis=3, concat_axis=4, tiled=True))
        coil_r = coils[:, 0]
        coil_i = coils[:, 1]
        sum_r = jnp.sum(map_r * coil_r + map_i * coil_i, axis=0)
        sum_i = jnp.sum(map_r * coil_i - map_i * coil_r, axis=0)
        return jnp.stack((sum_r, sum_i), 0)

    rhs_local = to_image(samples * weight)

    def total(local):
        return lax.psum(local, "coil")

    def inner(first, second):
        return lax.psum(jnp.sum(first * second), "slab")

    rhs = total(rhs_local)
    solution = jnp.zeros_like(rhs)
    residual = rhs
    direction = rhs
    norm_now = inner(residual, residual)
    for step in range(ITERS):
        sample_coil_r = map_r * direction[0][None] - map_i * direction[1][None]
        sample_coil_i = map_r * direction[1][None] + map_i * direction[0][None]
        spec_r, spec_i = transform(
            sample_coil_r, sample_coil_i, cos_y, sin_y, -1.0, "cxzn,nk->cxzk"
        )
        sample_spectra = jnp.stack((spec_r, spec_i), 1)
        forward_piece = lax.all_to_all(
            sample_spectra, "slab", split_axis=4, concat_axis=3, tiled=True
        )
        forward_out_r, forward_out_i = transform(
            forward_piece[:, 0], forward_piece[:, 1], cos_z, sin_z, -1.0, "cxzy,zk->cxyk"
        )
        sample_grid = jnp.stack((forward_out_r, forward_out_i), 1)
        blocks = sample_grid.reshape(ncoil, 2, nblocks, blocklen)
        picked = blocks[:, :, tile_block]
        image = (
            total(to_image(jnp.einsum("citb,ab->cita", picked, kernel, precision=HIGH) * weight))
            + SHIFT * direction
        )
        alpha = norm_now / inner(direction, image)
        solution = solution + alpha * direction
        residual = residual - alpha * image
        norm_next = inner(residual, residual)
        direction = residual + norm_next / norm_now * direction
        norm_now = norm_next
    return (solution, residual)


RADIX = 3
F32 = jnp.float32
BF16 = jnp.bfloat16
ROOT = math.sqrt(3.0) / 2.0


def split(value):
    high = value.astype(BF16)
    return high, (value - high.astype(F32)).astype(BF16)


def dot(left, right, form=((1,), (0,))):
    return lax.dot_general(left, right, (form, ((), ())), preferred_element_type=F32)


def dot_left(table_high, table_low, value, form=((1,), (0,))):
    high, low = split(value)
    return dot(table_high, high, form) + (dot(table_high, low, form) + dot(table_low, high, form))


def dot_right(value, table_high, table_low):
    high, low = split(value)
    return dot(high, table_high) + (dot(low, table_high) + dot(high, table_low))


def butterfly(parts, sign):
    (a_r, a_i), (b_r, b_i), (c_r, c_i) = parts
    sum_r, sum_i = b_r + c_r, b_i + c_i
    dif_r, dif_i = (sign * ROOT) * (b_r - c_r), (sign * ROOT) * (b_i - c_i)
    mid_r, mid_i = a_r - 0.5 * sum_r, a_i - 0.5 * sum_i
    return (
        (a_r + sum_r, a_i + sum_i),
        (mid_r - dif_i, mid_i + dif_r),
        (mid_r + dif_i, mid_i - dif_r),
    )


def dft_tables(length):
    base = length // RADIX
    index = np.arange(base)
    whole = np.arange(length)
    angle = (index[:, None] * whole[None, :] % length) * (2.0 * np.pi / length)
    real = np.cos(angle) / np.sqrt(length)
    imag = -np.sin(angle) / np.sqrt(length)
    tables = []
    for part in range(RADIX):
        re, im = real[:, part::RADIX], imag[:, part::RADIX]
        right = np.block([[re, im], [-im, re]])
        left = np.block([[re, -im], [im, re]])
        tables.append((left, left.T, right, right.T))
    full = np.array(tables, dtype=np.float32)
    high = full.astype(ml_dtypes.bfloat16)
    low = (full - high.astype(np.float32)).astype(ml_dtypes.bfloat16)
    return np.stack((high, low), 2)


def mark_blocks(info, marks):
    step = 128
    cells, tiles = marks.shape
    offset = (lax.axis_index("slab") % 2 * cells).astype(F32)
    column = info[0:1, :] - offset

    def fill(chunk, carry):
        start = pl.multiple_of(chunk * step, step)
        rows = lax.broadcasted_iota(jnp.int32, (step, tiles), 0) + start
        marks[pl.ds(start, step), :] = (rows.astype(F32) == column).astype(F32).astype(BF16)
        return carry

    lax.fori_loop(0, cells // step, fill, 0)


def add_blocks(back_high, back_low, marks, grid):
    step = 384

    def chunk(index, carry):
        start = pl.multiple_of(index * step, step)
        mark = marks[pl.ds(start, step), :]
        rows = ((1,), (1,))
        grid[:, pl.ds(start, step)] = dot(back_high[...], mark, rows) + dot(back_low[...], mark, rows)
        return carry

    lax.fori_loop(0, marks.shape[0] // step, chunk, 0)


def grid_to_image(grid, tables, middle, maps, out, ready=None):
    coils, _, _, base, length = maps.shape
    for c in range(coils):
        parts = []
        for q in range(RADIX):
            part = grid[2 * base * c : 2 * base * (c + 1), q * length : (q + 1) * length]
            parts.append((part[:base], part[base:]))
        for b, (re, im) in enumerate(butterfly(parts, 1.0)):
            value = jnp.concatenate((re, im), 0)
            middle[b, :, c * length : (c + 1) * length] = dot_left(tables[b, 1, 0], tables[b, 1, 1], value)

    if ready is not None:
        ready()

    def rows(b, carry):
        sums = [None] * RADIX
        for c in range(coils):
            parts = []
            for r in range(RADIX):
                start = c * length + r * base
                value = middle[b, :, start : start + base]
                value = jnp.concatenate((value[:base], value[base:]), 1)
                back = dot_right(value, tables[r, 3, 0], tables[r, 3, 1])
                parts.append((back[:, :base], back[:, base:]))
            for q, (re, im) in enumerate(butterfly(parts, 1.0)):
                lanes = slice(q * base, (q + 1) * base)
                map_r, map_i = maps[c, 0, b, :, lanes], maps[c, 1, b, :, lanes]
                term = (map_r * re + map_i * im, map_r * im - map_i * re)
                if c:
                    term = (sums[q][0] + term[0], sums[q][1] + term[1])
                sums[q] = term
        for q in range(RADIX):
            lanes = slice(q * base, (q + 1) * base)
            out[0, b, :, lanes], out[1, b, :, lanes] = sums[q]
        return carry

    lax.fori_loop(0, RADIX, rows, 0)


def image_to_grid(image, tables, middle, maps, grid_high, grid_low):
    coils, _, _, base, length = maps.shape

    def rows(b, carry):
        for c in range(coils):
            parts = []
            for q in range(RADIX):
                lanes = slice(q * base, (q + 1) * base)
                map_r, map_i = maps[c, 0, b, :, lanes], maps[c, 1, b, :, lanes]
                re, im = image[0, b, :, lanes], image[1, b, :, lanes]
                parts.append((map_r * re - map_i * im, map_r * im + map_i * re))
            for r, (re, im) in enumerate(butterfly(parts, -1.0)):
                value = dot_right(jnp.concatenate((re, im), 1), tables[r, 2, 0], tables[r, 2, 1])
                start = c * length + r * base
                middle[b, :base, start : start + base] = value[:, :base]
                middle[b, base:, start : start + base] = value[:, base:]
        return carry

    lax.fori_loop(0, RADIX, rows, 0)
    for c in range(coils):
        parts = []
        for b in range(RADIX):
            value = middle[b, :, c * length : (c + 1) * length]
            value = dot_left(tables[b, 0, 0], tables[b, 0, 1], value)
            parts.append((value[:base], value[base:]))
        for q, (re, im) in enumerate(butterfly(parts, -1.0)):
            high, low = split(jnp.concatenate((re, im), 0))
            rows_c, lanes = slice(2 * base * c, 2 * base * (c + 1)), slice(q * length, (q + 1) * length)
            grid_high[rows_c, lanes] = high
            grid_low[rows_c, lanes] = low


def rhs_kernel(near_maps, samples, weight, own_info, kernel, tables, out, maps, info, data, arrived,
               marks, back_high, back_low, middle, grid, send, recv):
    base = kernel.shape[0]
    shard_tiles = samples.shape[1]
    lines = near_maps.shape[4]
    slab = lax.axis_index("slab")
    far, near = slab // 2, slab % 2
    others = ((1 - far) * 2 + near, far * 2 + (1 - near), (1 - far) * 2 + (1 - near))
    barrier = pltpu.get_barrier_semaphore()
    for other in others:
        pl.semaphore_signal(barrier, inc=1, device_id={"slab": other}, device_id_type=pl.DeviceIdType.MESH)
    pl.semaphore_wait(barrier, len(others))

    sent = []

    def push(source, target, slot, other):
        copy = pltpu.make_async_remote_copy(
            src_ref=source,
            dst_ref=target,
            send_sem=send.at[slot],
            recv_sem=recv.at[slot],
            device_id={"slab": other},
            device_id_type=pl.DeviceIdType.MESH,
        )
        copy.start()
        sent.append(copy)
        return copy

    parts = samples.shape[0] // 2

    def tiles_of(shard):
        return pl.ds(pl.multiple_of(shard * shard_tiles, shard_tiles), shard_tiles)

    def lines_of(shard):
        return pl.ds(pl.multiple_of(shard * lines, lines), lines)

    mine = tiles_of(slab)
    info_copies = [push(own_info, arrived.at[slab], index, other) for index, other in enumerate(others)]
    for part in range(samples.shape[0]):
        staged_samples = samples[part] * weight[...]
        data[part // parts, part % parts, mine, :] = staged_samples
    far_copy = push(data.at[1 - far, :, mine, :], data.at[1 - far, :, mine, :], 3, others[0])
    near_copy = push(data.at[far, :, mine, :], data.at[far, :, mine, :], 4, others[1])
    map_copies = []
    for index in (2, 0, 1):
        other = others[index]
        map_copies.append(push(near_maps.at[other], maps.at[:, :, :, lines_of(slab), :], 6 + index, other))
    maps[:, :, :, lines_of(slab), :] = near_maps[slab]
    arrived[slab] = own_info[...]
    for copy in info_copies:
        copy.wait_recv()
    for shard in range(arrived.shape[0]):
        info[:, shard * shard_tiles : (shard + 1) * shard_tiles] = arrived[shard]
    mark_blocks(info, marks)
    far_copy.wait_recv()
    passed = data.at[far, :, tiles_of(others[0]), :]
    last_copy = push(passed, passed, 5, others[1])

    kernel_high, kernel_low = split(kernel[...].T)

    def grid_tiles(shard):
        at = tiles_of(shard)
        for part in range(parts):
            back = dot_left(kernel_high, kernel_low, data[far, part, at, :], ((1,), (1,)))
            high, low = split(back)
            back_high[part * base : (part + 1) * base, at] = high
            back_low[part * base : (part + 1) * base, at] = low

    grid_tiles(slab)
    grid_tiles(others[0])
    near_copy.wait_recv()
    grid_tiles(others[1])
    last_copy.wait_recv()
    grid_tiles(others[2])
    add_blocks(back_high, back_low, marks, grid)

    def ready():
        for copy in map_copies:
            copy.wait_recv()

    grid_to_image(grid, tables, middle, maps, out, ready)
    for copy in sent:
        copy.wait_send()


def normal_kernel(image, info, kernel, tables, maps, out, marks, back_high, back_low, middle, grid, grid_high, grid_low):
    base = kernel.shape[0]
    mark_blocks(info, marks)
    image_to_grid(image, tables, middle, maps, grid_high, grid_low)
    kernel_high, kernel_low = split(kernel[...])
    turned_high, turned_low = split(kernel[...].T)
    step = 256

    def sample(index, carry):
        start = pl.multiple_of(index * step, step)
        mark = marks[:, pl.ds(start, step)]
        picked = dot(grid_high[...], mark) + dot(grid_low[...], mark)
        position = lax.broadcasted_iota(jnp.int32, (base, step), 0).astype(F32)
        count, density = info[1:2, pl.ds(start, step)], info[2:3, pl.ds(start, step)]
        weight = jnp.where(position < count, density, 0.0)
        for part in range(picked.shape[0] // base):
            rows = slice(part * base, (part + 1) * base)
            value = dot_left(kernel_high, kernel_low, picked[rows]) * weight
            high, low = split(dot_left(turned_high, turned_low, value))
            back_high[rows, pl.ds(start, step)] = high
            back_low[rows, pl.ds(start, step)] = low
        return carry

    lax.fori_loop(0, marks.shape[1] // step, sample, 0)
    add_blocks(back_high, back_low, marks, grid)
    grid_to_image(grid, tables, middle, maps, out)


def work_space(map_shape, tiles):
    coils, _, _, base, length = map_shape
    cells = RADIX * length
    rows = 2 * base * coils
    return [
        pltpu.VMEM((cells, tiles), BF16),
        pltpu.VMEM((rows, tiles), BF16),
        pltpu.VMEM((rows, tiles), BF16),
        pltpu.VMEM((RADIX, 2 * base, coils * length), F32),
        pltpu.VMEM((rows, cells), F32),
    ], pltpu.VMEM((rows, cells), BF16)


def rhs_call(map_shape, tiles, slabs):
    coils, _, _, base, length = map_shape
    image = jax.ShapeDtypeStruct(map_shape[1:], F32)
    whole = jax.ShapeDtypeStruct(map_shape, F32)
    facts = jax.ShapeDtypeStruct((8, tiles), F32)
    memory = pl.BlockSpec(memory_space=pltpu.VMEM)
    scratch = [
        pltpu.VMEM((2, 2 * coils, tiles, base), F32),
        pltpu.VMEM((slabs, 8, tiles // slabs), F32),
    ]
    return pl.pallas_call(
        rhs_kernel,
        out_shape=(image, whole, facts),
        in_specs=[memory] * 6,
        out_specs=[memory] * 3,
        scratch_shapes=scratch + work_space(map_shape, tiles)[0] + [pltpu.SemaphoreType.DMA((9,))] * 2,
        compiler_params=pltpu.CompilerParams(
            collective_id=2, has_side_effects=True, vmem_limit_bytes=56 * 2**20
        ),
    )


def normal_call(map_shape, tiles):
    scratch, half = work_space(map_shape, tiles)
    return pl.pallas_call(
        normal_kernel,
        out_shape=jax.ShapeDtypeStruct(map_shape[1:], F32),
        in_specs=[pl.BlockSpec(memory_space=pltpu.VMEM)] * 5,
        out_specs=pl.BlockSpec(memory_space=pltpu.VMEM),
        scratch_shapes=scratch + [half, half],
        compiler_params=pltpu.CompilerParams(vmem_limit_bytes=56 * 2**20),
    )


CHUNKS = 4
STEP = 96


def combine(first, refs):
    if first:
        part, direction_out, norm_out, whole, landed, work, tile, send, recv = refs
    else:
        (part, direction, residual, answer, norm, direction_out, residual_out, answer_out, norm_out,
         whole, landed, work, tile, send, recv) = refs
    slab, coil = lax.axis_index("slab"), lax.axis_index("coil")
    core, chip, far, near = coil % 2, coil // 2, slab // 2, slab % 2
    partners = (
        {"coil": chip * 2 + (1 - core)},
        {"coil": (1 - chip) * 2 + core},
        {"slab": (1 - far) * 2 + near},
        {"slab": far * 2 + (1 - near)},
    )
    bits = (core, chip, far)
    barrier = pltpu.get_barrier_semaphore()
    for partner in partners:
        pl.semaphore_signal(barrier, inc=1, device_id=partner, device_id_type=pl.DeviceIdType.MESH)
    pl.semaphore_wait(barrier, len(partners))

    total = part.shape[0]
    size = total // CHUNKS
    sent = []

    def rows(start, count):
        return pl.ds(pl.multiple_of(start, 8), count)

    def push(source, target, slot, axis):
        copy = pltpu.make_async_remote_copy(
            src_ref=source,
            dst_ref=target,
            send_sem=send.at[slot],
            recv_sem=recv.at[slot],
            device_id=partners[axis],
            device_id_type=pl.DeviceIdType.MESH,
        )
        copy.start()
        sent.append(copy)
        return copy

    orders = [(0, 1, 2) if chunk % 2 == 0 else (0, 2, 1) for chunk in range(CHUNKS)]
    starts = [chunk * size for chunk in range(CHUNKS)]
    flying = [None] * CHUNKS
    place = [0, size // 2, size // 2 + size // 4]
    slots = [[None] * 3 for _ in range(CHUNKS)]
    for stage in range(4):
        for chunk in range(CHUNKS):
            count = size >> stage
            if stage:
                flying[chunk].wait_recv()
                mine = rows(starts[chunk], count)
                arrived = landed[chunk, place[stage - 1] : place[stage - 1] + count, :]
                held = part if stage == 1 else work
                goal = whole if stage == 3 else work
                goal[mine, :] = held[mine, :] + arrived
            if stage < 3:
                half = count // 2
                bit = bits[orders[chunk][stage]]
                other = starts[chunk] + (1 - bit) * half
                source = part if stage == 0 else work
                target = landed.at[chunk, pl.ds(place[stage], half), :]
                flying[chunk] = push(source.at[rows(other, half), :], target, chunk * 6 + stage, orders[chunk][stage])
                starts[chunk] = starts[chunk] + bit * half
    for stage in range(4):
        for chunk in range(CHUNKS):
            if stage:
                flying[chunk].wait_recv()
                axis = orders[chunk][3 - stage]
                starts[chunk] = starts[chunk] - bits[axis] * (size >> (4 - stage))
            if stage < 3:
                axis = orders[chunk][2 - stage]
                mine = whole.at[rows(starts[chunk], size >> (3 - stage)), :]
                flying[chunk] = push(mine, mine, chunk * 6 + 3 + stage, axis)

    for copy in sent:
        copy.wait_send()
    sent.clear()

    def exchange(value, index):
        tile[index, 0] = jnp.broadcast_to(value, tile.shape[2:])
        copy = push(tile.at[index, 0], tile.at[index, 1], CHUNKS * 6 + index, 3)
        copy.wait_recv()
        return (tile[index, 0] + tile[index, 1])[:1, :1]

    def sweep(body):
        def step(index, carry):
            return carry + body(rows(index * STEP, STEP))

        lanes = lax.fori_loop(0, total // STEP, step, jnp.zeros((8, part.shape[1]), F32))
        return jnp.sum(lanes, keepdims=True)

    def fold(value):
        return jnp.sum(value.reshape(-1, 8, value.shape[1]), 0)

    if first:

        def copy_out(at):
            value = whole[at, :]
            direction_out[at, :] = value
            return fold(value * value)

        norm_out[...] = jnp.broadcast_to(exchange(sweep(copy_out), 0), norm_out.shape)
    else:

        def meet(at):
            move = direction[at, :]
            image = whole[at, :] + SHIFT * move
            work[at, :] = image
            return fold(move * image)

        before = norm[:1, :1]
        alpha = before / exchange(sweep(meet), 0)

        def shrink(at):
            left = residual[at, :] - alpha * work[at, :]
            residual_out[at, :] = left
            answer_out[at, :] = answer[at, :] + alpha * direction[at, :]
            return fold(left * left)

        after = exchange(sweep(shrink), 1)
        beta = after / before

        def turn(index, carry):
            at = rows(index * STEP, STEP)
            direction_out[at, :] = residual_out[at, :] + beta * direction[at, :]
            return carry

        lax.fori_loop(0, total // STEP, turn, 0)
        norm_out[...] = jnp.broadcast_to(after, norm_out.shape)
    for copy in sent:
        copy.wait_send()


def first_kernel(*refs):
    combine(True, refs)


def next_kernel(*refs):
    combine(False, refs)


def combine_call(first, shape):
    image = jax.ShapeDtypeStruct(shape, F32)
    scalar = jax.ShapeDtypeStruct((8, 128), F32)
    copies = CHUNKS * 6 + 2
    memory = pl.BlockSpec(memory_space=pltpu.VMEM)
    return pl.pallas_call(
        first_kernel if first else next_kernel,
        out_shape=(image, scalar) if first else (image, image, image, scalar),
        in_specs=[memory] * (1 if first else 5),
        out_specs=[memory] * (2 if first else 4),
        scratch_shapes=[
            pltpu.VMEM(shape, F32),
            pltpu.VMEM((CHUNKS, shape[0] // CHUNKS, shape[1]), F32),
            pltpu.VMEM(shape, F32),
            pltpu.VMEM((2, 2, 8, 128), F32),
            pltpu.SemaphoreType.DMA((copies,)),
            pltpu.SemaphoreType.DMA((copies,)),
        ],
        compiler_params=pltpu.CompilerParams(
            collective_id=0 if first else 1, has_side_effects=True, vmem_limit_bytes=56 * 2**20
        ),
    )


def whole_coils(coil_maps, samples, kernel, tile_block, tile_count, dcf_level, dcf_table):
    ncoil, _, xpos, zdev, ylen = coil_maps.shape
    base = kernel.shape[0]
    slabs = lax.axis_size("slab")
    slab = lax.axis_index("slab")
    ky_dev = ylen // slabs
    lines = zdev // RADIX
    zblocks = zdev * slabs // base
    pairs = slabs // xpos
    group = ncoil // pairs

    near = coil_maps.reshape(pairs, group, 2, xpos, lines, RADIX, ylen).transpose(0, 3, 1, 2, 5, 4, 6)
    near = near.reshape(slabs, group, 2, RADIX, lines, ylen)
    data = samples.reshape(ncoil * 2, *samples.shape[2:])
    shard_tiles = tile_block.shape[0]
    tiles = shard_tiles * slabs
    ky = slab * ky_dev + tile_block // zblocks % ky_dev
    column = tile_block % zblocks * ylen + ky % RADIX * base + ky // RADIX
    column = column + tile_block // (zblocks * ky_dev) * (zblocks * ylen)
    levels = jnp.arange(dcf_table.shape[0], dtype=jnp.int32)
    density = jnp.sum(jnp.where(dcf_level[:, None] == levels[None, :], dcf_table[None, :], 0.0), axis=1)
    position = jnp.arange(base, dtype=jnp.int32)
    weight = jnp.where(position[None, :] < tile_count[:, None], density[:, None], 0.0)
    info = jnp.stack((column.astype(F32), tile_count.astype(F32), density))
    info = jnp.concatenate((info, jnp.zeros((5, shard_tiles), F32)))

    tables = jnp.asarray(dft_tables(ylen))
    shape = (group, 2, RADIX, base, ylen)
    flat = (2 * RADIX * base, ylen)

    partial, maps, info = rhs_call(shape, tiles, slabs)(near, data, weight, info, kernel, tables)
    direction, norm = combine_call(True, flat)(partial.reshape(flat))
    residual, answer = direction, jnp.zeros_like(direction)
    normal = normal_call(shape, tiles)
    update = combine_call(False, flat)
    for step in range(ITERS):
        partial = normal(direction.reshape(shape[1:]), info, kernel, tables, maps)
        direction, residual, answer, norm = update(partial.reshape(flat), direction, residual, answer, norm)

    both = jnp.stack((answer, residual)).reshape(2, 2, RADIX, base, ylen)
    partner = slab + 1 - 2 * (slab % 2)
    keep = lax.dynamic_slice_in_dim(both, slab * lines, lines, 3)
    give = lax.dynamic_slice_in_dim(both, partner * lines, lines, 3)
    take = lax.ppermute(give, "slab", [(index, index ^ 1) for index in range(slabs)])
    low = slab % 2 == 0
    both = jnp.stack((jnp.where(low, keep, take), jnp.where(low, take, keep)), 2)
    both = both.transpose(0, 1, 2, 4, 3, 5).reshape(2, 2, xpos, zdev, ylen)
    return both[0], both[1]


def fits(mesh, coil_maps, samples, kernel):
    slabs, coils = mesh.shape["slab"], mesh.shape["coil"]
    coil_dev = coil_maps.shape[0] // coils
    zlen, ylen = coil_maps.shape[3:]
    base = kernel.shape[0]
    return (
        coil_dev == slabs == coils == 4
        and coil_maps.shape[2] == 2
        and zlen == ylen == RADIX * base
        and base == 128
        and zlen % (slabs * RADIX) == 0
        and samples.shape[2] % 256 == 0
    )


def solution(mesh):
    placed = (
        P("coil", "scan", None, "slab", None),
        P("coil", "scan", "slab", None),
        P(),
        P("slab"),
        P("slab"),
        P("slab"),
        P(),
    )

    def run(coil_maps, samples, kernel, *rest):
        chosen = whole_coils if fits(mesh, coil_maps, samples, kernel) else body
        return jax.shard_map(
            chosen,
            mesh=mesh,
            in_specs=placed,
            out_specs=(P("scan", None, "slab", None), P("scan", None, "slab", None)),
            check_vma=False,
        )(coil_maps, samples, kernel, *rest)

    return run
```

```python
import math

import jax
import jax.numpy as jnp
import ml_dtypes
import numpy as np
from jax import lax
from jax.experimental import pallas as pl
from jax.experimental.pallas import tpu as pltpu
from jax.sharding import PartitionSpec as P

ITERS = 2


HIGH = lax.Precision.HIGHEST
SHIFT = 0.5


def tables(count):
    index = jnp.arange(count, dtype=jnp.int32)
    phase = index[:, None] * index[None, :] % count
    angle = phase.astype(jnp.float32) * (2.0 * math.pi / count)
    factor = 1.0 / math.sqrt(count)
    return (jnp.cos(angle) * factor, jnp.sin(angle) * factor)


def transform(real, imag, cosine, sine, sign, form):
    rc = jnp.einsum(form, real, cosine, precision=HIGH)
    rs = jnp.einsum(form, real, sine, precision=HIGH)
    mc = jnp.einsum(form, imag, cosine, precision=HIGH)
    ms = jnp.einsum(form, imag, sine, precision=HIGH)
    return (rc - sign * ms, mc + sign * rs)


def body(coil_maps, samples, kernel, tile_block, tile_count, dcf_level, dcf_table):
    ncoil, _, xpos, zdev, ylen = coil_maps.shape
    blocklen = kernel.shape[0]
    slabs = lax.axis_size("slab")
    zlen = zdev * slabs
    ky_dev = ylen // slabs
    nblocks = xpos * ky_dev * (zlen // blocklen)
    cos_y, sin_y = tables(ylen)
    cos_z, sin_z = tables(zlen)
    levels = jnp.arange(dcf_table.shape[0], dtype=jnp.int32)
    density = jnp.sum(
        jnp.where(dcf_level[:, None] == levels[None, :], dcf_table[None, :], 0.0), axis=1
    )
    valid = (jnp.arange(blocklen, dtype=jnp.int32)[None, :] < tile_count[:, None]).astype(
        jnp.float32
    )
    weight = density[:, None] * valid
    map_r = coil_maps[:, 0]
    map_i = coil_maps[:, 1]

    def inverse_y(piece):
        out_r, out_i = transform(piece[:, 0], piece[:, 1], cos_y, sin_y, 1.0, "cxzn,nk->cxzk")
        return jnp.stack((out_r, out_i), 1)

    def to_image(values):
        back = jnp.einsum("cita,ab->citb", values, kernel, precision=HIGH)
        blank = jnp.zeros((ncoil, 2, nblocks, blocklen), jnp.float32)
        grid = blank.at[:, :, tile_block].add(back).reshape(ncoil, 2, xpos, ky_dev, zlen)
        part_r, part_i = transform(grid[:, 0], grid[:, 1], cos_z, sin_z, 1.0, "cxyk,zk->cxzy")
        spectra = jnp.stack((part_r, part_i), 1)
        coils = inverse_y(lax.all_to_all(spectra, "slab", split_axis=3, concat_axis=4, tiled=True))
        coil_r = coils[:, 0]
        coil_i = coils[:, 1]
        sum_r = jnp.sum(map_r * coil_r + map_i * coil_i, axis=0)
        sum_i = jnp.sum(map_r * coil_i - map_i * coil_r, axis=0)
        return jnp.stack((sum_r, sum_i), 0)

    rhs_local = to_image(samples * weight)

    def total(local):
        return lax.psum(local, "coil")

    def inner(first, second):
        return lax.psum(jnp.sum(first * second), "slab")

    rhs = total(rhs_local)
    solution = jnp.zeros_like(rhs)
    residual = rhs
    direction = rhs
    norm_now = inner(residual, residual)
    for step in range(ITERS):
        sample_coil_r = map_r * direction[0][None] - map_i * direction[1][None]
        sample_coil_i = map_r * direction[1][None] + map_i * direction[0][None]
        spec_r, spec_i = transform(
            sample_coil_r, sample_coil_i, cos_y, sin_y, -1.0, "cxzn,nk->cxzk"
        )
        sample_spectra = jnp.stack((spec_r, spec_i), 1)
        forward_piece = lax.all_to_all(
            sample_spectra, "slab", split_axis=4, concat_axis=3, tiled=True
        )
        forward_out_r, forward_out_i = transform(
            forward_piece[:, 0], forward_piece[:, 1], cos_z, sin_z, -1.0, "cxzy,zk->cxyk"
        )
        sample_grid = jnp.stack((forward_out_r, forward_out_i), 1)
        blocks = sample_grid.reshape(ncoil, 2, nblocks, blocklen)
        picked = blocks[:, :, tile_block]
        image = (
            total(to_image(jnp.einsum("citb,ab->cita", picked, kernel, precision=HIGH) * weight))
            + SHIFT * direction
        )
        alpha = norm_now / inner(direction, image)
        solution = solution + alpha * direction
        residual = residual - alpha * image
        norm_next = inner(residual, residual)
        direction = residual + norm_next / norm_now * direction
        norm_now = norm_next
    return (solution, residual)


RADIX = 3
F32 = jnp.float32
BF16 = jnp.bfloat16
ROOT = math.sqrt(3.0) / 2.0


def split(value):
    high = value.astype(BF16)
    return high, (value - high.astype(F32)).astype(BF16)


def dot(left, right, form=((1,), (0,))):
    return lax.dot_general(left, right, (form, ((), ())), preferred_element_type=F32)


def dot_left(table_high, table_low, value, form=((1,), (0,))):
    high, low = split(value)
    return dot(table_high, high, form) + (dot(table_high, low, form) + dot(table_low, high, form))


def dot_right(value, table_high, table_low):
    high, low = split(value)
    return dot(high, table_high) + (dot(low, table_high) + dot(high, table_low))


def butterfly(parts, sign):
    (a_r, a_i), (b_r, b_i), (c_r, c_i) = parts
    sum_r, sum_i = b_r + c_r, b_i + c_i
    dif_r, dif_i = (sign * ROOT) * (b_r - c_r), (sign * ROOT) * (b_i - c_i)
    mid_r, mid_i = a_r - 0.5 * sum_r, a_i - 0.5 * sum_i
    return (
        (a_r + sum_r, a_i + sum_i),
        (mid_r - dif_i, mid_i + dif_r),
        (mid_r + dif_i, mid_i - dif_r),
    )


def dft_tables(length):
    base = length // RADIX
    index = np.arange(base)
    whole = np.arange(length)
    angle = (index[:, None] * whole[None, :] % length) * (2.0 * np.pi / length)
    real = np.cos(angle) / np.sqrt(length)
    imag = -np.sin(angle) / np.sqrt(length)
    tables = []
    for part in range(RADIX):
        re, im = real[:, part::RADIX], imag[:, part::RADIX]
        right = np.block([[re, im], [-im, re]])
        left = np.block([[re, -im], [im, re]])
        tables.append((left, left.T, right, right.T))
    full = np.array(tables, dtype=np.float32)
    high = full.astype(ml_dtypes.bfloat16)
    low = (full - high.astype(np.float32)).astype(ml_dtypes.bfloat16)
    return np.stack((high, low), 2)


def mark_blocks(info, marks):
    step = 128
    cells, tiles = marks.shape
    offset = (lax.axis_index("slab") % 2 * cells).astype(F32)
    column = info[0:1, :] - offset

    def fill(chunk, carry):
        start = pl.multiple_of(chunk * step, step)
        rows = lax.broadcasted_iota(jnp.int32, (step, tiles), 0) + start
        marks[pl.ds(start, step), :] = (rows.astype(F32) == column).astype(F32).astype(BF16)
        return carry

    lax.fori_loop(0, cells // step, fill, 0)


def add_blocks(back_high, back_low, marks, grid):
    step = 384

    def chunk(index, carry):
        start = pl.multiple_of(index * step, step)
        mark = marks[pl.ds(start, step), :]
        rows = ((1,), (1,))
        grid[:, pl.ds(start, step)] = dot(back_high[...], mark, rows) + dot(back_low[...], mark, rows)
        return carry

    lax.fori_loop(0, marks.shape[0] // step, chunk, 0)


def grid_to_image(grid, tables, middle, maps, out, ready=None):
    coils, _, _, base, length = maps.shape
    for c in range(coils):
        parts = []
        for q in range(RADIX):
            part = grid[2 * base * c : 2 * base * (c + 1), q * length : (q + 1) * length]
            parts.append((part[:base], part[base:]))
        for b, (re, im) in enumerate(butterfly(parts, 1.0)):
            value = jnp.concatenate((re, im), 0)
            middle[b, :, c * length : (c + 1) * length] = dot_left(tables[b, 1, 0], tables[b, 1, 1], value)

    if ready is not None:
        ready()

    def rows(b, carry):
        sums = [None] * RADIX
        for c in range(coils):
            parts = []
            for r in range(RADIX):
                start = c * length + r * base
                value = middle[b, :, start : start + base]
                value = jnp.concatenate((value[:base], value[base:]), 1)
                back = dot_right(value, tables[r, 3, 0], tables[r, 3, 1])
                parts.append((back[:, :base], back[:, base:]))
            for q, (re, im) in enumerate(butterfly(parts, 1.0)):
                lanes = slice(q * base, (q + 1) * base)
                map_r, map_i = maps[c, 0, b, :, lanes], maps[c, 1, b, :, lanes]
                term = (map_r * re + map_i * im, map_r * im - map_i * re)
                if c:
                    term = (sums[q][0] + term[0], sums[q][1] + term[1])
                sums[q] = term
        for q in range(RADIX):
            lanes = slice(q * base, (q + 1) * base)
            out[0, b, :, lanes], out[1, b, :, lanes] = sums[q]
        return carry

    lax.fori_loop(0, RADIX, rows, 0)


def image_to_grid(image, tables, middle, maps, grid_high, grid_low):
    coils, _, _, base, length = maps.shape

    def rows(b, carry):
        for c in range(coils):
            parts = []
            for q in range(RADIX):
                lanes = slice(q * base, (q + 1) * base)
                map_r, map_i = maps[c, 0, b, :, lanes], maps[c, 1, b, :, lanes]
                re, im = image[0, b, :, lanes], image[1, b, :, lanes]
                parts.append((map_r * re - map_i * im, map_r * im + map_i * re))
            for r, (re, im) in enumerate(butterfly(parts, -1.0)):
                value = dot_right(jnp.concatenate((re, im), 1), tables[r, 2, 0], tables[r, 2, 1])
                start = c * length + r * base
                middle[b, :base, start : start + base] = value[:, :base]
                middle[b, base:, start : start + base] = value[:, base:]
        return carry

    lax.fori_loop(0, RADIX, rows, 0)
    for c in range(coils):
        parts = []
        for b in range(RADIX):
            value = middle[b, :, c * length : (c + 1) * length]
            value = dot_left(tables[b, 0, 0], tables[b, 0, 1], value)
            parts.append((value[:base], value[base:]))
        for q, (re, im) in enumerate(butterfly(parts, -1.0)):
            high, low = split(jnp.concatenate((re, im), 0))
            rows_c, lanes = slice(2 * base * c, 2 * base * (c + 1)), slice(q * length, (q + 1) * length)
            grid_high[rows_c, lanes] = high
            grid_low[rows_c, lanes] = low


def rhs_kernel(near_maps, samples, weight, own_info, kernel, tables, out, maps, info, data, arrived,
               marks, back_high, back_low, middle, grid, send, recv):
    base = kernel.shape[0]
    shard_tiles = samples.shape[1]
    lines = near_maps.shape[5]
    slab = lax.axis_index("slab")
    far, near = slab // 2, slab % 2
    others = ((1 - far) * 2 + near, far * 2 + (1 - near), (1 - far) * 2 + (1 - near))
    barrier = pltpu.get_barrier_semaphore()
    for other in others:
        pl.semaphore_signal(barrier, inc=1, device_id={"slab": other}, device_id_type=pl.DeviceIdType.MESH)
    pl.semaphore_wait(barrier, len(others))

    sent = []

    def push(source, target, slot, other):
        copy = pltpu.make_async_remote_copy(
            src_ref=source,
            dst_ref=target,
            send_sem=send.at[slot],
            recv_sem=recv.at[slot],
            device_id={"slab": other},
            device_id_type=pl.DeviceIdType.MESH,
        )
        copy.start()
        sent.append(copy)
        return copy

    parts = samples.shape[0] // 2

    def tiles_of(shard):
        return pl.ds(pl.multiple_of(shard * shard_tiles, shard_tiles), shard_tiles)

    def lines_of(shard):
        return pl.ds(pl.multiple_of(shard * lines, lines), lines)

    mine = tiles_of(slab)
    info_copies = [push(own_info, arrived.at[slab], index, other) for index, other in enumerate(others)]
    for part in range(samples.shape[0]):
        staged_samples = samples[part] * weight[...]
        data[part // parts, part % parts, mine, :] = staged_samples
    far_copy = push(data.at[1 - far, :, mine, :], data.at[1 - far, :, mine, :], 3, others[0])
    near_copy = push(data.at[far, :, mine, :], data.at[far, :, mine, :], 4, others[1])
    map_copies = []
    for index in (2, 0, 1):
        other = others[index]
        map_copies.append(push(near_maps.at[other // 2, :, :, other % 2], maps.at[:, :, :, lines_of(slab), :], 6 + index, other))
    maps[:, :, :, lines_of(slab), :] = near_maps[far, :, :, near]
    arrived[slab] = own_info[...]
    for copy in info_copies:
        copy.wait_recv()
    for shard in range(arrived.shape[0]):
        info[:, shard * shard_tiles : (shard + 1) * shard_tiles] = arrived[shard]
    mark_blocks(info, marks)
    far_copy.wait_recv()
    passed = data.at[far, :, tiles_of(others[0]), :]
    last_copy = push(passed, passed, 5, others[1])

    kernel_high, kernel_low = split(kernel[...].T)

    def grid_tiles(shard):
        at = tiles_of(shard)
        for part in range(parts):
            back = dot_left(kernel_high, kernel_low, data[far, part, at, :], ((1,), (1,)))
            high, low = split(back)
            back_high[part * base : (part + 1) * base, at] = high
            back_low[part * base : (part + 1) * base, at] = low

    grid_tiles(slab)
    grid_tiles(others[0])
    near_copy.wait_recv()
    grid_tiles(others[1])
    last_copy.wait_recv()
    grid_tiles(others[2])
    add_blocks(back_high, back_low, marks, grid)

    def ready():
        for copy in map_copies:
            copy.wait_recv()

    grid_to_image(grid, tables, middle, maps, out, ready)
    for copy in sent:
        copy.wait_send()


def normal_kernel(image, info, kernel, tables, maps, out, marks, back_high, back_low, middle, grid, grid_high, grid_low):
    base = kernel.shape[0]
    mark_blocks(info, marks)
    image_to_grid(image, tables, middle, maps, grid_high, grid_low)
    kernel_high, kernel_low = split(kernel[...])
    turned_high, turned_low = split(kernel[...].T)
    step = 256

    def sample(index, carry):
        start = pl.multiple_of(index * step, step)
        mark = marks[:, pl.ds(start, step)]
        picked = dot(grid_high[...], mark) + dot(grid_low[...], mark)
        position = lax.broadcasted_iota(jnp.int32, (base, step), 0).astype(F32)
        count, density = info[1:2, pl.ds(start, step)], info[2:3, pl.ds(start, step)]
        weight = jnp.where(position < count, density, 0.0)
        for part in range(picked.shape[0] // base):
            rows = slice(part * base, (part + 1) * base)
            value = dot_left(kernel_high, kernel_low, picked[rows]) * weight
            high, low = split(dot_left(turned_high, turned_low, value))
            back_high[rows, pl.ds(start, step)] = high
            back_low[rows, pl.ds(start, step)] = low
        return carry

    lax.fori_loop(0, marks.shape[1] // step, sample, 0)
    add_blocks(back_high, back_low, marks, grid)
    grid_to_image(grid, tables, middle, maps, out)


def work_space(map_shape, tiles):
    coils, _, _, base, length = map_shape
    cells = RADIX * length
    rows = 2 * base * coils
    return [
        pltpu.VMEM((cells, tiles), BF16),
        pltpu.VMEM((rows, tiles), BF16),
        pltpu.VMEM((rows, tiles), BF16),
        pltpu.VMEM((RADIX, 2 * base, coils * length), F32),
        pltpu.VMEM((rows, cells), F32),
    ], pltpu.VMEM((rows, cells), BF16)


def rhs_call(map_shape, tiles, slabs):
    coils, _, _, base, length = map_shape
    image = jax.ShapeDtypeStruct(map_shape[1:], F32)
    whole = jax.ShapeDtypeStruct(map_shape, F32)
    facts = jax.ShapeDtypeStruct((8, tiles), F32)
    memory = pl.BlockSpec(memory_space=pltpu.VMEM)
    scratch = [
        pltpu.VMEM((2, 2 * coils, tiles, base), F32),
        pltpu.VMEM((slabs, 8, tiles // slabs), F32),
    ]
    return pl.pallas_call(
        rhs_kernel,
        out_shape=(image, whole, facts),
        in_specs=[memory] * 6,
        out_specs=[memory] * 3,
        scratch_shapes=scratch + work_space(map_shape, tiles)[0] + [pltpu.SemaphoreType.DMA((9,))] * 2,
        compiler_params=pltpu.CompilerParams(
            collective_id=2, has_side_effects=True, vmem_limit_bytes=56 * 2**20
        ),
    )


def normal_call(map_shape, tiles):
    scratch, half = work_space(map_shape, tiles)
    return pl.pallas_call(
        normal_kernel,
        out_shape=jax.ShapeDtypeStruct(map_shape[1:], F32),
        in_specs=[pl.BlockSpec(memory_space=pltpu.VMEM)] * 5,
        out_specs=pl.BlockSpec(memory_space=pltpu.VMEM),
        scratch_shapes=scratch + [half, half],
        compiler_params=pltpu.CompilerParams(vmem_limit_bytes=56 * 2**20),
    )


CHUNKS = 4
STEP = 96


def combine(first, refs):
    if first:
        part, direction_out, norm_out, whole, landed, work, tile, send, recv = refs
    else:
        (part, direction, residual, answer, norm, direction_out, residual_out, answer_out, norm_out,
         whole, landed, work, tile, send, recv) = refs
    slab, coil = lax.axis_index("slab"), lax.axis_index("coil")
    core, chip, far, near = coil % 2, coil // 2, slab // 2, slab % 2
    partners = (
        {"coil": chip * 2 + (1 - core)},
        {"coil": (1 - chip) * 2 + core},
        {"slab": (1 - far) * 2 + near},
        {"slab": far * 2 + (1 - near)},
    )
    bits = (core, chip, far)
    barrier = pltpu.get_barrier_semaphore()
    for partner in partners:
        pl.semaphore_signal(barrier, inc=1, device_id=partner, device_id_type=pl.DeviceIdType.MESH)
    pl.semaphore_wait(barrier, len(partners))

    total = part.shape[0]
    size = total // CHUNKS
    sent = []

    def rows(start, count):
        return pl.ds(pl.multiple_of(start, 8), count)

    def push(source, target, slot, axis):
        copy = pltpu.make_async_remote_copy(
            src_ref=source,
            dst_ref=target,
            send_sem=send.at[slot],
            recv_sem=recv.at[slot],
            device_id=partners[axis],
            device_id_type=pl.DeviceIdType.MESH,
        )
        copy.start()
        sent.append(copy)
        return copy

    starts = [chunk * size for chunk in range(CHUNKS)]
    flying = [None] * CHUNKS
    place = [0, size // 2, size // 2 + size // 4]

    def advance(chunk, stage):
        if stage:
            flying[chunk].wait_recv()
        if 1 <= stage <= 3:
            count = size >> stage
            mine = rows(starts[chunk], count)
            arrived = landed[chunk, place[stage - 1] : place[stage - 1] + count, :]
            held = part if stage == 1 else work
            goal = whole if stage == 3 else work
            goal[mine, :] = held[mine, :] + arrived
        if stage < 3:
            half = size >> (stage + 1)
            other = starts[chunk] + (1 - bits[stage]) * half
            source = part if stage == 0 else work
            target = landed.at[chunk, pl.ds(place[stage], half), :]
            flying[chunk] = push(source.at[rows(other, half), :], target, chunk * 6 + stage, stage)
            starts[chunk] = starts[chunk] + bits[stage] * half
        else:
            if stage > 3:
                starts[chunk] = starts[chunk] - bits[6 - stage] * (size >> (7 - stage))
            if stage < 6:
                mine = whole.at[rows(starts[chunk], size >> (6 - stage)), :]
                flying[chunk] = push(mine, mine, chunk * 6 + stage, 5 - stage)

    for front in range(7 + CHUNKS - 1):
        for chunk in range(CHUNKS):
            if 0 <= front - chunk < 7:
                advance(chunk, front - chunk)
    for copy in sent:
        copy.wait_send()
    sent.clear()

    def exchange(value, index):
        tile[index, 0] = jnp.broadcast_to(value, tile.shape[2:])
        copy = push(tile.at[index, 0], tile.at[index, 1], CHUNKS * 6 + index, 3)
        copy.wait_recv()
        return (tile[index, 0] + tile[index, 1])[:1, :1]

    def sweep(body):
        def step(index, carry):
            return carry + body(rows(index * STEP, STEP))

        lanes = lax.fori_loop(0, total // STEP, step, jnp.zeros((8, part.shape[1]), F32))
        return jnp.sum(lanes, keepdims=True)

    def fold(value):
        return jnp.sum(value.reshape(-1, 8, value.shape[1]), 0)

    if first:

        def copy_out(at):
            value = whole[at, :]
            direction_out[at, :] = value
            return fold(value * value)

        norm_out[...] = jnp.broadcast_to(exchange(sweep(copy_out), 0), norm_out.shape)
    else:

        def meet(at):
            move = direction[at, :]
            image = whole[at, :] + SHIFT * move
            work[at, :] = image
            return fold(move * image)

        before = norm[:1, :1]
        alpha = before / exchange(sweep(meet), 0)

        def shrink(at):
            left = residual[at, :] - alpha * work[at, :]
            residual_out[at, :] = left
            answer_out[at, :] = answer[at, :] + alpha * direction[at, :]
            return fold(left * left)

        after = exchange(sweep(shrink), 1)
        beta = after / before

        def turn(index, carry):
            at = rows(index * STEP, STEP)
            direction_out[at, :] = residual_out[at, :] + beta * direction[at, :]
            return carry

        lax.fori_loop(0, total // STEP, turn, 0)
        norm_out[...] = jnp.broadcast_to(after, norm_out.shape)
    for copy in sent:
        copy.wait_send()


def first_kernel(*refs):
    combine(True, refs)


def next_kernel(*refs):
    combine(False, refs)


def combine_call(first, shape):
    image = jax.ShapeDtypeStruct(shape, F32)
    scalar = jax.ShapeDtypeStruct((8, 128), F32)
    copies = CHUNKS * 6 + 2
    memory = pl.BlockSpec(memory_space=pltpu.VMEM)
    return pl.pallas_call(
        first_kernel if first else next_kernel,
        out_shape=(image, scalar) if first else (image, image, image, scalar),
        in_specs=[memory] * (1 if first else 5),
        out_specs=[memory] * (2 if first else 4),
        scratch_shapes=[
            pltpu.VMEM(shape, F32),
            pltpu.VMEM((CHUNKS, shape[0] // CHUNKS, shape[1]), F32),
            pltpu.VMEM(shape, F32),
            pltpu.VMEM((2, 2, 8, 128), F32),
            pltpu.SemaphoreType.DMA((copies,)),
            pltpu.SemaphoreType.DMA((copies,)),
        ],
        compiler_params=pltpu.CompilerParams(
            collective_id=0 if first else 1, has_side_effects=True, vmem_limit_bytes=56 * 2**20
        ),
    )


def whole_coils(coil_maps, samples, kernel, tile_block, tile_count, dcf_level, dcf_table):
    ncoil, _, xpos, zdev, ylen = coil_maps.shape
    base = kernel.shape[0]
    slabs = lax.axis_size("slab")
    slab = lax.axis_index("slab")
    ky_dev = ylen // slabs
    lines = zdev // RADIX
    zblocks = zdev * slabs // base
    pairs = slabs // xpos
    group = ncoil // pairs

    near = coil_maps.reshape(pairs, group, 2, xpos, lines, RADIX, ylen).transpose(0, 1, 2, 3, 5, 4, 6)
    data = samples.reshape(ncoil * 2, *samples.shape[2:])
    shard_tiles = tile_block.shape[0]
    tiles = shard_tiles * slabs
    ky = slab * ky_dev + tile_block // zblocks % ky_dev
    column = tile_block % zblocks * ylen + ky % RADIX * base + ky // RADIX
    column = column + tile_block // (zblocks * ky_dev) * (zblocks * ylen)
    levels = jnp.arange(dcf_table.shape[0], dtype=jnp.int32)
    density = jnp.sum(jnp.where(dcf_level[:, None] == levels[None, :], dcf_table[None, :], 0.0), axis=1)
    position = jnp.arange(base, dtype=jnp.int32)
    weight = jnp.where(position[None, :] < tile_count[:, None], density[:, None], 0.0)
    info = jnp.stack((column.astype(F32), tile_count.astype(F32), density))
    info = jnp.concatenate((info, jnp.zeros((5, shard_tiles), F32)))

    tables = jnp.asarray(dft_tables(ylen))
    shape = (group, 2, RADIX, base, ylen)
    flat = (2 * RADIX * base, ylen)

    partial, maps, info = rhs_call(shape, tiles, slabs)(near, data, weight, info, kernel, tables)
    direction, norm = combine_call(True, flat)(partial.reshape(flat))
    residual, answer = direction, jnp.zeros_like(direction)
    normal = normal_call(shape, tiles)
    update = combine_call(False, flat)
    for step in range(ITERS):
        partial = normal(direction.reshape(shape[1:]), info, kernel, tables, maps)
        direction, residual, answer, norm = update(partial.reshape(flat), direction, residual, answer, norm)

    both = jnp.stack((answer, residual)).reshape(2, 2, RADIX, base, ylen)
    partner = slab + 1 - 2 * (slab % 2)
    keep = lax.dynamic_slice_in_dim(both, slab * lines, lines, 3)
    give = lax.dynamic_slice_in_dim(both, partner * lines, lines, 3)
    take = lax.ppermute(give, "slab", [(index, index ^ 1) for index in range(slabs)])
    low = slab % 2 == 0
    both = jnp.stack((jnp.where(low, keep, take), jnp.where(low, take, keep)), 2)
    both = both.transpose(0, 1, 2, 4, 3, 5).reshape(2, 2, xpos, zdev, ylen)
    return both[0], both[1]


def fits(mesh, coil_maps, samples, kernel):
    slabs, coils = mesh.shape["slab"], mesh.shape["coil"]
    coil_dev = coil_maps.shape[0] // coils
    zlen, ylen = coil_maps.shape[3:]
    base = kernel.shape[0]
    return (
        coil_dev == slabs == coils == 4
        and coil_maps.shape[2] == 2
        and zlen == ylen == RADIX * base
        and base == 128
        and zlen % (slabs * RADIX) == 0
        and samples.shape[2] % 256 == 0
    )


def solution(mesh):
    placed = (
        P("coil", "scan", None, "slab", None),
        P("coil", "scan", "slab", None),
        P(),
        P("slab"),
        P("slab"),
        P("slab"),
        P(),
    )

    def run(coil_maps, samples, kernel, *rest):
        chosen = whole_coils if fits(mesh, coil_maps, samples, kernel) else body
        return jax.shard_map(
            chosen,
            mesh=mesh,
            in_specs=placed,
            out_specs=(P("scan", None, "slab", None), P("scan", None, "slab", None)),
            check_vma=False,
        )(coil_maps, samples, kernel, *rest)

    return run
```

```python
import math

import jax
import jax.numpy as jnp
import ml_dtypes
import numpy as np
from jax import lax
from jax.experimental import pallas as pl
from jax.experimental.pallas import tpu as pltpu
from jax.sharding import PartitionSpec as P

ITERS = 2


HIGH = lax.Precision.HIGHEST
SHIFT = 0.5


def tables(count):
    index = jnp.arange(count, dtype=jnp.int32)
    phase = index[:, None] * index[None, :] % count
    angle = phase.astype(jnp.float32) * (2.0 * math.pi / count)
    factor = 1.0 / math.sqrt(count)
    return (jnp.cos(angle) * factor, jnp.sin(angle) * factor)


def transform(real, imag, cosine, sine, sign, form):
    rc = jnp.einsum(form, real, cosine, precision=HIGH)
    rs = jnp.einsum(form, real, sine, precision=HIGH)
    mc = jnp.einsum(form, imag, cosine, precision=HIGH)
    ms = jnp.einsum(form, imag, sine, precision=HIGH)
    return (rc - sign * ms, mc + sign * rs)


def body(coil_maps, samples, kernel, tile_block, tile_count, dcf_level, dcf_table):
    ncoil, _, xpos, zdev, ylen = coil_maps.shape
    blocklen = kernel.shape[0]
    slabs = lax.axis_size("slab")
    zlen = zdev * slabs
    ky_dev = ylen // slabs
    nblocks = xpos * ky_dev * (zlen // blocklen)
    cos_y, sin_y = tables(ylen)
    cos_z, sin_z = tables(zlen)
    levels = jnp.arange(dcf_table.shape[0], dtype=jnp.int32)
    density = jnp.sum(
        jnp.where(dcf_level[:, None] == levels[None, :], dcf_table[None, :], 0.0), axis=1
    )
    valid = (jnp.arange(blocklen, dtype=jnp.int32)[None, :] < tile_count[:, None]).astype(
        jnp.float32
    )
    weight = density[:, None] * valid
    map_r = coil_maps[:, 0]
    map_i = coil_maps[:, 1]

    def inverse_y(piece):
        out_r, out_i = transform(piece[:, 0], piece[:, 1], cos_y, sin_y, 1.0, "cxzn,nk->cxzk")
        return jnp.stack((out_r, out_i), 1)

    def to_image(values):
        back = jnp.einsum("cita,ab->citb", values, kernel, precision=HIGH)
        blank = jnp.zeros((ncoil, 2, nblocks, blocklen), jnp.float32)
        grid = blank.at[:, :, tile_block].add(back).reshape(ncoil, 2, xpos, ky_dev, zlen)
        part_r, part_i = transform(grid[:, 0], grid[:, 1], cos_z, sin_z, 1.0, "cxyk,zk->cxzy")
        spectra = jnp.stack((part_r, part_i), 1)
        coils = inverse_y(lax.all_to_all(spectra, "slab", split_axis=3, concat_axis=4, tiled=True))
        coil_r = coils[:, 0]
        coil_i = coils[:, 1]
        sum_r = jnp.sum(map_r * coil_r + map_i * coil_i, axis=0)
        sum_i = jnp.sum(map_r * coil_i - map_i * coil_r, axis=0)
        return jnp.stack((sum_r, sum_i), 0)

    rhs_local = to_image(samples * weight)

    def total(local):
        return lax.psum(local, "coil")

    def inner(first, second):
        return lax.psum(jnp.sum(first * second), "slab")

    rhs = total(rhs_local)
    solution = jnp.zeros_like(rhs)
    residual = rhs
    direction = rhs
    norm_now = inner(residual, residual)
    for step in range(ITERS):
        sample_coil_r = map_r * direction[0][None] - map_i * direction[1][None]
        sample_coil_i = map_r * direction[1][None] + map_i * direction[0][None]
        spec_r, spec_i = transform(
            sample_coil_r, sample_coil_i, cos_y, sin_y, -1.0, "cxzn,nk->cxzk"
        )
        sample_spectra = jnp.stack((spec_r, spec_i), 1)
        forward_piece = lax.all_to_all(
            sample_spectra, "slab", split_axis=4, concat_axis=3, tiled=True
        )
        forward_out_r, forward_out_i = transform(
            forward_piece[:, 0], forward_piece[:, 1], cos_z, sin_z, -1.0, "cxzy,zk->cxyk"
        )
        sample_grid = jnp.stack((forward_out_r, forward_out_i), 1)
        blocks = sample_grid.reshape(ncoil, 2, nblocks, blocklen)
        picked = blocks[:, :, tile_block]
        image = (
            total(to_image(jnp.einsum("citb,ab->cita", picked, kernel, precision=HIGH) * weight))
            + SHIFT * direction
        )
        alpha = norm_now / inner(direction, image)
        solution = solution + alpha * direction
        residual = residual - alpha * image
        norm_next = inner(residual, residual)
        direction = residual + norm_next / norm_now * direction
        norm_now = norm_next
    return (solution, residual)


RADIX = 3
F32 = jnp.float32
BF16 = jnp.bfloat16
ROOT = math.sqrt(3.0) / 2.0


def split(value):
    high = value.astype(BF16)
    return high, (value - high.astype(F32)).astype(BF16)


def dot(left, right, form=((1,), (0,))):
    return lax.dot_general(left, right, (form, ((), ())), preferred_element_type=F32)


def dot_left(table_high, table_low, value, form=((1,), (0,))):
    high, low = split(value)
    return dot(table_high, high, form) + (dot(table_high, low, form) + dot(table_low, high, form))


def dot_right(value, table_high, table_low):
    high, low = split(value)
    return dot(high, table_high) + (dot(low, table_high) + dot(high, table_low))


def butterfly(parts, sign):
    (a_r, a_i), (b_r, b_i), (c_r, c_i) = parts
    sum_r, sum_i = b_r + c_r, b_i + c_i
    dif_r, dif_i = (sign * ROOT) * (b_r - c_r), (sign * ROOT) * (b_i - c_i)
    mid_r, mid_i = a_r - 0.5 * sum_r, a_i - 0.5 * sum_i
    return (
        (a_r + sum_r, a_i + sum_i),
        (mid_r - dif_i, mid_i + dif_r),
        (mid_r + dif_i, mid_i - dif_r),
    )


def dft_tables(length):
    base = length // RADIX
    index = np.arange(base)
    whole = np.arange(length)
    angle = (index[:, None] * whole[None, :] % length) * (2.0 * np.pi / length)
    real = np.cos(angle) / np.sqrt(length)
    imag = -np.sin(angle) / np.sqrt(length)
    tables = []
    for part in range(RADIX):
        re, im = real[:, part::RADIX], imag[:, part::RADIX]
        right = np.block([[re, im], [-im, re]])
        left = np.block([[re, -im], [im, re]])
        tables.append((left, left.T, right, right.T))
    full = np.array(tables, dtype=np.float32)
    high = full.astype(ml_dtypes.bfloat16)
    low = (full - high.astype(np.float32)).astype(ml_dtypes.bfloat16)
    return np.stack((high, low), 2)


def mark_blocks(info, marks):
    step = 128
    cells, tiles = marks.shape
    offset = (lax.axis_index("slab") % 2 * cells).astype(F32)
    column = info[0:1, :] - offset

    def fill(chunk, carry):
        start = pl.multiple_of(chunk * step, step)
        rows = lax.broadcasted_iota(jnp.int32, (step, tiles), 0) + start
        marks[pl.ds(start, step), :] = (rows.astype(F32) == column).astype(F32).astype(BF16)
        return carry

    lax.fori_loop(0, cells // step, fill, 0)


def add_blocks(back_high, back_low, marks, grid):
    step = 384

    def chunk(index, carry):
        start = pl.multiple_of(index * step, step)
        mark = marks[pl.ds(start, step), :]
        rows = ((1,), (1,))
        grid[:, pl.ds(start, step)] = dot(back_high[...], mark, rows) + dot(back_low[...], mark, rows)
        return carry

    lax.fori_loop(0, marks.shape[0] // step, chunk, 0)


def image_rows(part, b, base):
    return pl.ds(pl.multiple_of((part * RADIX + b) * base, base), base)


def grid_to_image(grid, tables, middle, maps, out, ready=None):
    coils, _, _, base, length = maps.shape
    for c in range(coils):
        parts = []
        for q in range(RADIX):
            part = grid[2 * base * c : 2 * base * (c + 1), q * length : (q + 1) * length]
            parts.append((part[:base], part[base:]))
        for b, (re, im) in enumerate(butterfly(parts, 1.0)):
            value = jnp.concatenate((re, im), 0)
            middle[b, :, c * length : (c + 1) * length] = dot_left(tables[b, 1, 0], tables[b, 1, 1], value)

    if ready is not None:
        ready()

    def rows(b, carry):
        sums = [None] * RADIX
        for c in range(coils):
            parts = []
            for r in range(RADIX):
                start = c * length + r * base
                value = middle[b, :, start : start + base]
                value = jnp.concatenate((value[:base], value[base:]), 1)
                back = dot_right(value, tables[r, 3, 0], tables[r, 3, 1])
                parts.append((back[:, :base], back[:, base:]))
            for q, (re, im) in enumerate(butterfly(parts, 1.0)):
                lanes = slice(q * base, (q + 1) * base)
                map_r, map_i = maps[c, 0, b, :, lanes], maps[c, 1, b, :, lanes]
                term = (map_r * re + map_i * im, map_r * im - map_i * re)
                if c:
                    term = (sums[q][0] + term[0], sums[q][1] + term[1])
                sums[q] = term
        for q in range(RADIX):
            lanes = slice(q * base, (q + 1) * base)
            out[image_rows(0, b, base), lanes], out[image_rows(1, b, base), lanes] = sums[q]
        return carry

    lax.fori_loop(0, RADIX, rows, 0)


def image_to_grid(image, tables, middle, maps, grid_high, grid_low):
    coils, _, _, base, length = maps.shape

    def rows(b, carry):
        for c in range(coils):
            parts = []
            for q in range(RADIX):
                lanes = slice(q * base, (q + 1) * base)
                map_r, map_i = maps[c, 0, b, :, lanes], maps[c, 1, b, :, lanes]
                re, im = image[image_rows(0, b, base), lanes], image[image_rows(1, b, base), lanes]
                parts.append((map_r * re - map_i * im, map_r * im + map_i * re))
            for r, (re, im) in enumerate(butterfly(parts, -1.0)):
                value = dot_right(jnp.concatenate((re, im), 1), tables[r, 2, 0], tables[r, 2, 1])
                start = c * length + r * base
                middle[b, :base, start : start + base] = value[:, :base]
                middle[b, base:, start : start + base] = value[:, base:]
        return carry

    lax.fori_loop(0, RADIX, rows, 0)
    for c in range(coils):
        parts = []
        for b in range(RADIX):
            value = middle[b, :, c * length : (c + 1) * length]
            value = dot_left(tables[b, 0, 0], tables[b, 0, 1], value)
            parts.append((value[:base], value[base:]))
        for q, (re, im) in enumerate(butterfly(parts, -1.0)):
            high, low = split(jnp.concatenate((re, im), 0))
            rows_c, lanes = slice(2 * base * c, 2 * base * (c + 1)), slice(q * length, (q + 1) * length)
            grid_high[rows_c, lanes] = high
            grid_low[rows_c, lanes] = low


def adjoint_of_samples(near_maps, samples, weight, own_info, kernel, tables, out, maps, info, data, arrived,
               marks, back_high, back_low, middle, grid, send, recv):
    base = kernel.shape[0]
    shard_tiles = samples.shape[1]
    lines = near_maps.shape[5]
    slab = lax.axis_index("slab")
    far, near = slab // 2, slab % 2
    others = ((1 - far) * 2 + near, far * 2 + (1 - near), (1 - far) * 2 + (1 - near))
    sent = []

    def push(source, target, slot, other):
        copy = pltpu.make_async_remote_copy(
            src_ref=source,
            dst_ref=target,
            send_sem=send.at[slot],
            recv_sem=recv.at[slot],
            device_id={"slab": other},
            device_id_type=pl.DeviceIdType.MESH,
        )
        copy.start()
        sent.append(copy)
        return copy

    parts = samples.shape[0] // 2

    def tiles_of(shard):
        return pl.ds(pl.multiple_of(shard * shard_tiles, shard_tiles), shard_tiles)

    def lines_of(shard):
        return pl.ds(pl.multiple_of(shard * lines, lines), lines)

    mine = tiles_of(slab)
    info_copies = [push(own_info, arrived.at[slab], index, other) for index, other in enumerate(others)]
    for part in range(samples.shape[0]):
        staged_samples = samples[part] * weight[...]
        data[part // parts, part % parts, mine, :] = staged_samples
    far_copy = push(data.at[1 - far, :, mine, :], data.at[1 - far, :, mine, :], 3, others[0])
    near_copy = push(data.at[far, :, mine, :], data.at[far, :, mine, :], 4, others[1])
    map_copies = []
    for index in (2, 0, 1):
        other = others[index]
        map_copies.append(push(near_maps.at[other // 2, :, :, other % 2], maps.at[:, :, :, lines_of(slab), :], 6 + index, other))
    maps[:, :, :, lines_of(slab), :] = near_maps[far, :, :, near]
    arrived[slab] = own_info[...]
    for copy in info_copies:
        copy.wait_recv()
    for shard in range(arrived.shape[0]):
        info[:, shard * shard_tiles : (shard + 1) * shard_tiles] = arrived[shard]
    mark_blocks(info, marks)
    far_copy.wait_recv()
    passed = data.at[far, :, tiles_of(others[0]), :]
    last_copy = push(passed, passed, 5, others[1])

    kernel_high, kernel_low = split(kernel[...].T)

    def grid_tiles(shard):
        at = tiles_of(shard)
        for part in range(parts):
            back = dot_left(kernel_high, kernel_low, data[far, part, at, :], ((1,), (1,)))
            high, low = split(back)
            back_high[part * base : (part + 1) * base, at] = high
            back_low[part * base : (part + 1) * base, at] = low

    grid_tiles(slab)
    grid_tiles(others[0])
    near_copy.wait_recv()
    grid_tiles(others[1])
    last_copy.wait_recv()
    grid_tiles(others[2])
    add_blocks(back_high, back_low, marks, grid)

    def ready():
        for copy in map_copies:
            copy.wait_recv()

    grid_to_image(grid, tables, middle, maps, out, ready)
    for copy in sent:
        copy.wait_send()


def normal(image, info, kernel, tables, maps, out, marks, back_high, back_low, middle, grid, grid_high, grid_low):
    base = kernel.shape[0]
    image_to_grid(image, tables, middle, maps, grid_high, grid_low)
    kernel_high, kernel_low = split(kernel[...])
    turned_high, turned_low = split(kernel[...].T)
    step = 256

    def sample(index, carry):
        start = pl.multiple_of(index * step, step)
        mark = marks[:, pl.ds(start, step)]
        picked = dot(grid_high[...], mark) + dot(grid_low[...], mark)
        position = lax.broadcasted_iota(jnp.int32, (base, step), 0).astype(F32)
        count, density = info[1:2, pl.ds(start, step)], info[2:3, pl.ds(start, step)]
        weight = jnp.where(position < count, density, 0.0)
        for part in range(picked.shape[0] // base):
            rows = slice(part * base, (part + 1) * base)
            value = dot_left(kernel_high, kernel_low, picked[rows]) * weight
            high, low = split(dot_left(turned_high, turned_low, value))
            back_high[rows, pl.ds(start, step)] = high
            back_low[rows, pl.ds(start, step)] = low
        return carry

    lax.fori_loop(0, marks.shape[1] // step, sample, 0)
    add_blocks(back_high, back_low, marks, grid)
    grid_to_image(grid, tables, middle, maps, out)


CHUNKS = 4
STEP = 96


def combine(turn_index, part, direction, residual, answer, norm, whole, landed, work, tile, send, recv):
    first = turn_index == 0
    base_slot = turn_index * (CHUNKS * 6 + 2)
    slab, coil = lax.axis_index("slab"), lax.axis_index("coil")
    core, chip, far, near = coil % 2, coil // 2, slab // 2, slab % 2
    partners = (
        {"coil": chip * 2 + (1 - core)},
        {"coil": (1 - chip) * 2 + core},
        {"slab": (1 - far) * 2 + near},
        {"slab": far * 2 + (1 - near)},
    )
    bits = (core, chip, far)
    total = part.shape[0]
    size = total // CHUNKS
    sent = []

    def rows(start, count):
        return pl.ds(pl.multiple_of(start, 8), count)

    def push(source, target, slot, axis):
        copy = pltpu.make_async_remote_copy(
            src_ref=source,
            dst_ref=target,
            send_sem=send.at[base_slot + slot],
            recv_sem=recv.at[base_slot + slot],
            device_id=partners[axis],
            device_id_type=pl.DeviceIdType.MESH,
        )
        copy.start()
        sent.append(copy)
        return copy

    orders = [(0, 1, 2) if chunk % 2 == 0 else (0, 2, 1) for chunk in range(CHUNKS)]
    starts = [chunk * size for chunk in range(CHUNKS)]
    flying = [None] * CHUNKS
    place = [0, size // 2, size // 2 + size // 4]
    slots = [[None] * 3 for _ in range(CHUNKS)]
    for stage in range(4):
        for chunk in range(CHUNKS):
            count = size >> stage
            if stage:
                flying[chunk].wait_recv()
                mine = rows(starts[chunk], count)
                arrived = landed[chunk, place[stage - 1] : place[stage - 1] + count, :]
                held = part if stage == 1 else work
                goal = whole if stage == 3 else work
                goal[mine, :] = held[mine, :] + arrived
            if stage < 3:
                half = count // 2
                bit = bits[orders[chunk][stage]]
                other = starts[chunk] + (1 - bit) * half
                source = part if stage == 0 else work
                target = landed.at[chunk, pl.ds(place[stage], half), :]
                flying[chunk] = push(source.at[rows(other, half), :], target, chunk * 6 + stage, orders[chunk][stage])
                starts[chunk] = starts[chunk] + bit * half
    for stage in range(4):
        for chunk in range(CHUNKS):
            if stage:
                flying[chunk].wait_recv()
                axis = orders[chunk][3 - stage]
                starts[chunk] = starts[chunk] - bits[axis] * (size >> (4 - stage))
            if stage < 3:
                axis = orders[chunk][2 - stage]
                mine = whole.at[rows(starts[chunk], size >> (3 - stage)), :]
                flying[chunk] = push(mine, mine, chunk * 6 + 3 + stage, axis)

    for copy in sent:
        copy.wait_send()
    sent.clear()

    def exchange(value, index):
        slot = turn_index * 2 + index
        tile[slot, 0] = jnp.broadcast_to(value, tile.shape[2:])
        copy = push(tile.at[slot, 0], tile.at[slot, 1], CHUNKS * 6 + index, 3)
        copy.wait_recv()
        return (tile[slot, 0] + tile[slot, 1])[:1, :1]

    def sweep(body):
        def step(index, carry):
            return carry + body(rows(index * STEP, STEP))

        lanes = lax.fori_loop(0, total // STEP, step, jnp.zeros((8, part.shape[1]), F32))
        return jnp.sum(lanes, keepdims=True)

    def fold(value):
        return jnp.sum(value.reshape(-1, 8, value.shape[1]), 0)

    if first:

        def copy_out(at):
            value = whole[at, :]
            direction[at, :] = value
            residual[at, :] = value
            answer[at, :] = jnp.zeros_like(value)
            return fold(value * value)

        norm[...] = jnp.broadcast_to(exchange(sweep(copy_out), 0), norm.shape)
    else:

        def meet(at):
            move = direction[at, :]
            image = whole[at, :] + SHIFT * move
            work[at, :] = image
            return fold(move * image)

        before = norm[:1, :1]
        alpha = before / exchange(sweep(meet), 0)

        def shrink(at):
            left = residual[at, :] - alpha * work[at, :]
            residual[at, :] = left
            answer[at, :] = answer[at, :] + alpha * direction[at, :]
            return fold(left * left)

        after = exchange(sweep(shrink), 1)
        beta = after / before

        def turn(index, carry):
            at = rows(index * STEP, STEP)
            direction[at, :] = residual[at, :] + beta * direction[at, :]
            return carry

        lax.fori_loop(0, total // STEP, turn, 0)
        norm[...] = jnp.broadcast_to(after, norm.shape)
    for copy in sent:
        copy.wait_send()


def whole_kernel(near_maps, samples, weight, own_info, kernel, tables, answer, residual, maps, info, data, arrived,
                 marks, back_high, back_low, middle, grid, grid_high, grid_low, part, direction, norm, whole, landed,
                 work, tile, map_send, map_recv, send, recv):
    slab, coil = lax.axis_index("slab"), lax.axis_index("coil")
    core, chip, far, near = coil % 2, coil // 2, slab // 2, slab % 2
    partners = (
        {"coil": chip * 2 + (1 - core)},
        {"coil": (1 - chip) * 2 + core},
        {"slab": (1 - far) * 2 + near},
        {"slab": far * 2 + (1 - near)},
        {"slab": (1 - far) * 2 + (1 - near)},
    )
    barrier = pltpu.get_barrier_semaphore()
    for partner in partners:
        pl.semaphore_signal(barrier, inc=1, device_id=partner, device_id_type=pl.DeviceIdType.MESH)
    pl.semaphore_wait(barrier, len(partners))
    space = (marks, back_high, back_low, middle, grid)
    sums = (part, direction, residual, answer, norm, whole, landed, work, tile, send, recv)
    adjoint_of_samples(near_maps, samples, weight, own_info, kernel, tables, part, maps, info, data, arrived,
                       *space, map_send, map_recv)
    combine(0, *sums)
    for step in range(ITERS):
        normal(direction, info, kernel, tables, maps, part, *space, grid_high, grid_low)
        combine(step + 1, *sums)


def whole_call(map_shape, tiles, slabs):
    coils, _, _, base, length = map_shape
    cells = RADIX * length
    rows = 2 * base * coils
    flat = (2 * RADIX * base, length)
    copies = (ITERS + 1) * (CHUNKS * 6 + 2)
    image = pltpu.VMEM(flat, F32)
    memory = pl.BlockSpec(memory_space=pltpu.VMEM)
    return pl.pallas_call(
        whole_kernel,
        out_shape=(jax.ShapeDtypeStruct(flat, F32), jax.ShapeDtypeStruct(flat, F32)),
        in_specs=[memory] * 6,
        out_specs=[memory] * 2,
        scratch_shapes=[
            pltpu.VMEM(map_shape, F32),
            pltpu.VMEM((8, tiles), F32),
            pltpu.VMEM((2, 2 * coils, tiles, base), F32),
            pltpu.VMEM((slabs, 8, tiles // slabs), F32),
            pltpu.VMEM((cells, tiles), BF16),
            pltpu.VMEM((rows, tiles), BF16),
            pltpu.VMEM((rows, tiles), BF16),
            pltpu.VMEM((RADIX, 2 * base, coils * length), F32),
            pltpu.VMEM((rows, cells), F32),
            pltpu.VMEM((rows, cells), BF16),
            pltpu.VMEM((rows, cells), BF16),
            image,
            image,
            pltpu.VMEM((8, 128), F32),
            image,
            pltpu.VMEM((CHUNKS, flat[0] // CHUNKS, length), F32),
            image,
            pltpu.VMEM((2 * ITERS + 2, 2, 8, 128), F32),
            pltpu.SemaphoreType.DMA((9,)),
            pltpu.SemaphoreType.DMA((9,)),
            pltpu.SemaphoreType.DMA((copies,)),
            pltpu.SemaphoreType.DMA((copies,)),
        ],
        compiler_params=pltpu.CompilerParams(
            collective_id=0, has_side_effects=True, vmem_limit_bytes=60 * 2**20
        ),
    )


def whole_coils(coil_maps, samples, kernel, tile_block, tile_count, dcf_level, dcf_table):
    ncoil, _, xpos, zdev, ylen = coil_maps.shape
    base = kernel.shape[0]
    slabs = lax.axis_size("slab")
    slab = lax.axis_index("slab")
    ky_dev = ylen // slabs
    lines = zdev // RADIX
    zblocks = zdev * slabs // base
    pairs = slabs // xpos
    group = ncoil // pairs

    near = coil_maps.reshape(pairs, group, 2, xpos, lines, RADIX, ylen).transpose(0, 1, 2, 3, 5, 4, 6)
    data = samples.reshape(ncoil * 2, *samples.shape[2:])
    shard_tiles = tile_block.shape[0]
    tiles = shard_tiles * slabs
    ky = slab * ky_dev + tile_block // zblocks % ky_dev
    column = tile_block % zblocks * ylen + ky % RADIX * base + ky // RADIX
    column = column + tile_block // (zblocks * ky_dev) * (zblocks * ylen)
    levels = jnp.arange(dcf_table.shape[0], dtype=jnp.int32)
    density = jnp.sum(jnp.where(dcf_level[:, None] == levels[None, :], dcf_table[None, :], 0.0), axis=1)
    position = jnp.arange(base, dtype=jnp.int32)
    weight = jnp.where(position[None, :] < tile_count[:, None], density[:, None], 0.0)
    info = jnp.stack((column.astype(F32), tile_count.astype(F32), density))
    info = jnp.concatenate((info, jnp.zeros((5, shard_tiles), F32)))

    tables = jnp.asarray(dft_tables(ylen))
    shape = (group, 2, RADIX, base, ylen)
    answer, residual = whole_call(shape, tiles, slabs)(near, data, weight, info, kernel, tables)

    both = jnp.stack((answer, residual)).reshape(2, 2, RADIX, base, ylen)
    partner = slab + 1 - 2 * (slab % 2)
    keep = lax.dynamic_slice_in_dim(both, slab * lines, lines, 3)
    give = lax.dynamic_slice_in_dim(both, partner * lines, lines, 3)
    take = lax.ppermute(give, "slab", [(index, index ^ 1) for index in range(slabs)])
    low = slab % 2 == 0
    both = jnp.stack((jnp.where(low, keep, take), jnp.where(low, take, keep)), 2)
    both = both.transpose(0, 1, 2, 4, 3, 5).reshape(2, 2, xpos, zdev, ylen)
    return both[0], both[1]


def fits(mesh, coil_maps, samples, kernel):
    slabs, coils = mesh.shape["slab"], mesh.shape["coil"]
    coil_dev = coil_maps.shape[0] // coils
    zlen, ylen = coil_maps.shape[3:]
    base = kernel.shape[0]
    return (
        coil_dev == slabs == coils == 4
        and coil_maps.shape[2] == 2
        and zlen == ylen == RADIX * base
        and base == 128
        and zlen % (slabs * RADIX) == 0
        and samples.shape[2] % 256 == 0
    )


def solution(mesh):
    placed = (
        P("coil", "scan", None, "slab", None),
        P("coil", "scan", "slab", None),
        P(),
        P("slab"),
        P("slab"),
        P("slab"),
        P(),
    )

    def run(coil_maps, samples, kernel, *rest):
        chosen = whole_coils if fits(mesh, coil_maps, samples, kernel) else body
        return jax.shard_map(
            chosen,
            mesh=mesh,
            in_specs=placed,
            out_specs=(P("scan", None, "slab", None), P("scan", None, "slab", None)),
            check_vma=False,
        )(coil_maps, samples, kernel, *rest)

    return run
```

```python
import math

import jax
import jax.numpy as jnp
import ml_dtypes
import numpy as np
from jax import lax
from jax.experimental import pallas as pl
from jax.experimental.pallas import tpu as pltpu
from jax.sharding import PartitionSpec as P

ITERS = 2


HIGH = lax.Precision.HIGHEST
SHIFT = 0.5


def tables(count):
    index = jnp.arange(count, dtype=jnp.int32)
    phase = index[:, None] * index[None, :] % count
    angle = phase.astype(jnp.float32) * (2.0 * math.pi / count)
    factor = 1.0 / math.sqrt(count)
    return (jnp.cos(angle) * factor, jnp.sin(angle) * factor)


def transform(real, imag, cosine, sine, sign, form):
    rc = jnp.einsum(form, real, cosine, precision=HIGH)
    rs = jnp.einsum(form, real, sine, precision=HIGH)
    mc = jnp.einsum(form, imag, cosine, precision=HIGH)
    ms = jnp.einsum(form, imag, sine, precision=HIGH)
    return (rc - sign * ms, mc + sign * rs)


def body(coil_maps, samples, kernel, tile_block, tile_count, dcf_level, dcf_table):
    ncoil, _, xpos, zdev, ylen = coil_maps.shape
    blocklen = kernel.shape[0]
    slabs = lax.axis_size("slab")
    zlen = zdev * slabs
    ky_dev = ylen // slabs
    nblocks = xpos * ky_dev * (zlen // blocklen)
    cos_y, sin_y = tables(ylen)
    cos_z, sin_z = tables(zlen)
    levels = jnp.arange(dcf_table.shape[0], dtype=jnp.int32)
    density = jnp.sum(
        jnp.where(dcf_level[:, None] == levels[None, :], dcf_table[None, :], 0.0), axis=1
    )
    valid = (jnp.arange(blocklen, dtype=jnp.int32)[None, :] < tile_count[:, None]).astype(
        jnp.float32
    )
    weight = density[:, None] * valid
    map_r = coil_maps[:, 0]
    map_i = coil_maps[:, 1]

    def inverse_y(piece):
        out_r, out_i = transform(piece[:, 0], piece[:, 1], cos_y, sin_y, 1.0, "cxzn,nk->cxzk")
        return jnp.stack((out_r, out_i), 1)

    def to_image(values):
        back = jnp.einsum("cita,ab->citb", values, kernel, precision=HIGH)
        blank = jnp.zeros((ncoil, 2, nblocks, blocklen), jnp.float32)
        grid = blank.at[:, :, tile_block].add(back).reshape(ncoil, 2, xpos, ky_dev, zlen)
        part_r, part_i = transform(grid[:, 0], grid[:, 1], cos_z, sin_z, 1.0, "cxyk,zk->cxzy")
        spectra = jnp.stack((part_r, part_i), 1)
        coils = inverse_y(lax.all_to_all(spectra, "slab", split_axis=3, concat_axis=4, tiled=True))
        coil_r = coils[:, 0]
        coil_i = coils[:, 1]
        sum_r = jnp.sum(map_r * coil_r + map_i * coil_i, axis=0)
        sum_i = jnp.sum(map_r * coil_i - map_i * coil_r, axis=0)
        return jnp.stack((sum_r, sum_i), 0)

    rhs_local = to_image(samples * weight)

    def total(local):
        return lax.psum(local, "coil")

    def inner(first, second):
        return lax.psum(jnp.sum(first * second), "slab")

    rhs = total(rhs_local)
    solution = jnp.zeros_like(rhs)
    residual = rhs
    direction = rhs
    norm_now = inner(residual, residual)
    for step in range(ITERS):
        sample_coil_r = map_r * direction[0][None] - map_i * direction[1][None]
        sample_coil_i = map_r * direction[1][None] + map_i * direction[0][None]
        spec_r, spec_i = transform(
            sample_coil_r, sample_coil_i, cos_y, sin_y, -1.0, "cxzn,nk->cxzk"
        )
        sample_spectra = jnp.stack((spec_r, spec_i), 1)
        forward_piece = lax.all_to_all(
            sample_spectra, "slab", split_axis=4, concat_axis=3, tiled=True
        )
        forward_out_r, forward_out_i = transform(
            forward_piece[:, 0], forward_piece[:, 1], cos_z, sin_z, -1.0, "cxzy,zk->cxyk"
        )
        sample_grid = jnp.stack((forward_out_r, forward_out_i), 1)
        blocks = sample_grid.reshape(ncoil, 2, nblocks, blocklen)
        picked = blocks[:, :, tile_block]
        image = (
            total(to_image(jnp.einsum("citb,ab->cita", picked, kernel, precision=HIGH) * weight))
            + SHIFT * direction
        )
        alpha = norm_now / inner(direction, image)
        solution = solution + alpha * direction
        residual = residual - alpha * image
        norm_next = inner(residual, residual)
        direction = residual + norm_next / norm_now * direction
        norm_now = norm_next
    return (solution, residual)


RADIX = 3
F32 = jnp.float32
BF16 = jnp.bfloat16
ROOT = math.sqrt(3.0) / 2.0


def split(value):
    high = value.astype(BF16)
    return high, (value - high.astype(F32)).astype(BF16)


def dot(left, right, form=((1,), (0,))):
    return lax.dot_general(left, right, (form, ((), ())), preferred_element_type=F32)


def dot_left(table_high, table_low, value, form=((1,), (0,))):
    high, low = split(value)
    return dot(table_high, high, form) + (dot(table_high, low, form) + dot(table_low, high, form))


def dot_right(value, table_high, table_low):
    high, low = split(value)
    return dot(high, table_high) + (dot(low, table_high) + dot(high, table_low))


def butterfly(parts, sign):
    (a_r, a_i), (b_r, b_i), (c_r, c_i) = parts
    sum_r, sum_i = b_r + c_r, b_i + c_i
    dif_r, dif_i = (sign * ROOT) * (b_r - c_r), (sign * ROOT) * (b_i - c_i)
    mid_r, mid_i = a_r - 0.5 * sum_r, a_i - 0.5 * sum_i
    return (
        (a_r + sum_r, a_i + sum_i),
        (mid_r - dif_i, mid_i + dif_r),
        (mid_r + dif_i, mid_i - dif_r),
    )


def dft_tables(length):
    base = length // RADIX
    index = np.arange(base)
    whole = np.arange(length)
    angle = (index[:, None] * whole[None, :] % length) * (2.0 * np.pi / length)
    real = np.cos(angle) / np.sqrt(length)
    imag = -np.sin(angle) / np.sqrt(length)
    tables = []
    for part in range(RADIX):
        re, im = real[:, part::RADIX], imag[:, part::RADIX]
        right = np.block([[re, im], [-im, re]])
        left = np.block([[re, -im], [im, re]])
        tables.append((left, left.T, right, right.T))
    full = np.array(tables, dtype=np.float32)
    high = full.astype(ml_dtypes.bfloat16)
    low = (full - high.astype(np.float32)).astype(ml_dtypes.bfloat16)
    return np.stack((high, low), 2)


def mark_blocks(info, marks):
    step = 128
    cells, tiles = marks.shape
    offset = (lax.axis_index("slab") % 2 * cells).astype(F32)
    column = info[0:1, :] - offset

    def fill(chunk, carry):
        start = pl.multiple_of(chunk * step, step)
        rows = lax.broadcasted_iota(jnp.int32, (step, tiles), 0) + start
        marks[pl.ds(start, step), :] = (rows.astype(F32) == column).astype(F32).astype(BF16)
        return carry

    lax.fori_loop(0, cells // step, fill, 0)


def add_blocks(back_high, back_low, marks, grid):
    step = 384

    def chunk(index, carry):
        start = pl.multiple_of(index * step, step)
        mark = marks[pl.ds(start, step), :]
        rows = ((1,), (1,))
        grid[:, pl.ds(start, step)] = dot(back_high[...], mark, rows) + dot(back_low[...], mark, rows)
        return carry

    lax.fori_loop(0, marks.shape[0] // step, chunk, 0)


def image_rows(part, b, base):
    return pl.ds(pl.multiple_of((part * RADIX + b) * base, base), base)


def grid_to_image(grid, tables, middle, maps, out, ready=None):
    coils, _, _, base, length = maps.shape
    for c in range(coils):
        parts = []
        for q in range(RADIX):
            part = grid[2 * base * c : 2 * base * (c + 1), q * length : (q + 1) * length]
            parts.append((part[:base], part[base:]))
        for b, (re, im) in enumerate(butterfly(parts, 1.0)):
            value = jnp.concatenate((re, im), 0)
            middle[b, :, c * length : (c + 1) * length] = dot_left(tables[b, 1, 0], tables[b, 1, 1], value)

    if ready is not None:
        ready()

    def rows(b, carry):
        sums = [None] * RADIX
        for c in range(coils):
            parts = []
            for r in range(RADIX):
                start = c * length + r * base
                value = middle[b, :, start : start + base]
                value = jnp.concatenate((value[:base], value[base:]), 1)
                back = dot_right(value, tables[r, 3, 0], tables[r, 3, 1])
                parts.append((back[:, :base], back[:, base:]))
            for q, (re, im) in enumerate(butterfly(parts, 1.0)):
                lanes = slice(q * base, (q + 1) * base)
                map_r, map_i = maps[c, 0, b, :, lanes], maps[c, 1, b, :, lanes]
                term = (map_r * re + map_i * im, map_r * im - map_i * re)
                if c:
                    term = (sums[q][0] + term[0], sums[q][1] + term[1])
                sums[q] = term
        for q in range(RADIX):
            lanes = slice(q * base, (q + 1) * base)
            out[image_rows(0, b, base), lanes], out[image_rows(1, b, base), lanes] = sums[q]
        return carry

    lax.fori_loop(0, RADIX, rows, 0)


def image_to_grid(image, tables, middle, maps, grid_high, grid_low):
    coils, _, _, base, length = maps.shape

    def rows(b, carry):
        for c in range(coils):
            parts = []
            for q in range(RADIX):
                lanes = slice(q * base, (q + 1) * base)
                map_r, map_i = maps[c, 0, b, :, lanes], maps[c, 1, b, :, lanes]
                re, im = image[image_rows(0, b, base), lanes], image[image_rows(1, b, base), lanes]
                parts.append((map_r * re - map_i * im, map_r * im + map_i * re))
            for r, (re, im) in enumerate(butterfly(parts, -1.0)):
                value = dot_right(jnp.concatenate((re, im), 1), tables[r, 2, 0], tables[r, 2, 1])
                start = c * length + r * base
                middle[b, :base, start : start + base] = value[:, :base]
                middle[b, base:, start : start + base] = value[:, base:]
        return carry

    lax.fori_loop(0, RADIX, rows, 0)
    for c in range(coils):
        parts = []
        for b in range(RADIX):
            value = middle[b, :, c * length : (c + 1) * length]
            value = dot_left(tables[b, 0, 0], tables[b, 0, 1], value)
            parts.append((value[:base], value[base:]))
        for q, (re, im) in enumerate(butterfly(parts, -1.0)):
            high, low = split(jnp.concatenate((re, im), 0))
            rows_c, lanes = slice(2 * base * c, 2 * base * (c + 1)), slice(q * length, (q + 1) * length)
            grid_high[rows_c, lanes] = high
            grid_low[rows_c, lanes] = low


def adjoint_of_samples(near_maps, samples, weight, own_info, kernel, tables, out, maps, info, data, arrived,
               marks, back_high, back_low, middle, grid, send, recv):
    base = kernel.shape[0]
    shard_tiles = samples.shape[1]
    lines = near_maps.shape[5]
    slab = lax.axis_index("slab")
    far, near = slab // 2, slab % 2
    others = ((1 - far) * 2 + near, far * 2 + (1 - near), (1 - far) * 2 + (1 - near))
    sent = []

    def push(source, target, slot, other):
        copy = pltpu.make_async_remote_copy(
            src_ref=source,
            dst_ref=target,
            send_sem=send.at[slot],
            recv_sem=recv.at[slot],
            device_id={"slab": other},
            device_id_type=pl.DeviceIdType.MESH,
        )
        copy.start()
        sent.append(copy)
        return copy

    parts = samples.shape[0] // 2

    def tiles_of(shard):
        return pl.ds(pl.multiple_of(shard * shard_tiles, shard_tiles), shard_tiles)

    def lines_of(shard):
        return pl.ds(pl.multiple_of(shard * lines, lines), lines)

    mine = tiles_of(slab)
    info_copies = [push(own_info, arrived.at[slab], index, other) for index, other in enumerate(others)]
    for part in range(samples.shape[0]):
        staged_samples = samples[part] * weight[...]
        data[part // parts, part % parts, mine, :] = staged_samples
    far_copy = push(data.at[1 - far, :, mine, :], data.at[1 - far, :, mine, :], 3, others[0])
    near_copy = push(data.at[far, :, mine, :], data.at[far, :, mine, :], 4, others[1])
    map_copies = []
    for index in (2, 0, 1):
        other = others[index]
        map_copies.append(push(near_maps.at[other // 2, :, :, other % 2], maps.at[:, :, :, lines_of(slab), :], 6 + index, other))
    maps[:, :, :, lines_of(slab), :] = near_maps[far, :, :, near]
    arrived[slab] = own_info[...]
    for copy in info_copies:
        copy.wait_recv()
    for shard in range(arrived.shape[0]):
        info[:, shard * shard_tiles : (shard + 1) * shard_tiles] = arrived[shard]
    mark_blocks(info, marks)
    far_copy.wait_recv()
    passed = data.at[far, :, tiles_of(others[0]), :]
    last_copy = push(passed, passed, 5, others[1])

    kernel_high, kernel_low = split(kernel[...].T)

    def grid_tiles(shard):
        at = tiles_of(shard)
        for part in range(parts):
            back = dot_left(kernel_high, kernel_low, data[far, part, at, :], ((1,), (1,)))
            high, low = split(back)
            back_high[part * base : (part + 1) * base, at] = high
            back_low[part * base : (part + 1) * base, at] = low

    grid_tiles(slab)
    grid_tiles(others[0])
    near_copy.wait_recv()
    grid_tiles(others[1])
    last_copy.wait_recv()
    grid_tiles(others[2])
    add_blocks(back_high, back_low, marks, grid)

    def ready():
        for copy in map_copies:
            copy.wait_recv()

    grid_to_image(grid, tables, middle, maps, out, ready)
    for copy in sent:
        copy.wait_send()


def normal(image, info, kernel, tables, maps, out, marks, back_high, back_low, middle, grid, grid_high, grid_low):
    base = kernel.shape[0]
    image_to_grid(image, tables, middle, maps, grid_high, grid_low)
    kernel_high, kernel_low = split(kernel[...])
    turned_high, turned_low = split(kernel[...].T)
    step = 256

    def sample(index, carry):
        start = pl.multiple_of(index * step, step)
        mark = marks[:, pl.ds(start, step)]
        picked = dot(grid_high[...], mark) + dot(grid_low[...], mark)
        position = lax.broadcasted_iota(jnp.int32, (base, step), 0).astype(F32)
        count, density = info[1:2, pl.ds(start, step)], info[2:3, pl.ds(start, step)]
        weight = jnp.where(position < count, density, 0.0)
        for part in range(picked.shape[0] // base):
            rows = slice(part * base, (part + 1) * base)
            value = dot_left(kernel_high, kernel_low, picked[rows]) * weight
            high, low = split(dot_left(turned_high, turned_low, value))
            back_high[rows, pl.ds(start, step)] = high
            back_low[rows, pl.ds(start, step)] = low
        return carry

    lax.fori_loop(0, marks.shape[1] // step, sample, 0)
    add_blocks(back_high, back_low, marks, grid)
    grid_to_image(grid, tables, middle, maps, out)


CHUNKS = 4
STEP = 96


def combine(turn_index, part, direction, residual, answer, norm, whole, landed, work, tile, send, recv):
    first = turn_index == 0
    base_slot = turn_index * (CHUNKS * 6 + 2)
    slab, coil = lax.axis_index("slab"), lax.axis_index("coil")
    core, chip, far, near = coil % 2, coil // 2, slab // 2, slab % 2
    partners = (
        {"coil": chip * 2 + (1 - core)},
        {"coil": (1 - chip) * 2 + core},
        {"slab": (1 - far) * 2 + near},
        {"slab": far * 2 + (1 - near)},
    )
    bits = (core, chip, far)
    total = part.shape[0]
    size = total // CHUNKS
    sent = []

    def rows(start, count):
        return pl.ds(pl.multiple_of(start, 8), count)

    def push(source, target, slot, axis):
        copy = pltpu.make_async_remote_copy(
            src_ref=source,
            dst_ref=target,
            send_sem=send.at[base_slot + slot],
            recv_sem=recv.at[base_slot + slot],
            device_id=partners[axis],
            device_id_type=pl.DeviceIdType.MESH,
        )
        copy.start()
        sent.append(copy)
        return copy

    orders = [(0, 1, 2) if chunk % 2 == 0 else (0, 2, 1) for chunk in range(CHUNKS)]
    starts = [chunk * size for chunk in range(CHUNKS)]
    flying = [None] * CHUNKS
    place = [0, size // 2, size // 2 + size // 4]
    slots = [[None] * 3 for _ in range(CHUNKS)]
    for stage in range(4):
        for chunk in range(CHUNKS):
            count = size >> stage
            if stage:
                flying[chunk].wait_recv()
                mine = rows(starts[chunk], count)
                arrived = landed[chunk, place[stage - 1] : place[stage - 1] + count, :]
                held = part if stage == 1 else work
                goal = whole if stage == 3 else work
                goal[mine, :] = held[mine, :] + arrived
            if stage < 3:
                half = count // 2
                bit = bits[orders[chunk][stage]]
                other = starts[chunk] + (1 - bit) * half
                source = part if stage == 0 else work
                target = landed.at[chunk, pl.ds(place[stage], half), :]
                flying[chunk] = push(source.at[rows(other, half), :], target, chunk * 6 + stage, orders[chunk][stage])
                starts[chunk] = starts[chunk] + bit * half
    for stage in range(4):
        for chunk in range(CHUNKS):
            if stage:
                flying[chunk].wait_recv()
                axis = orders[chunk][3 - stage]
                starts[chunk] = starts[chunk] - bits[axis] * (size >> (4 - stage))
            if stage < 3:
                axis = orders[chunk][2 - stage]
                mine = whole.at[rows(starts[chunk], size >> (3 - stage)), :]
                flying[chunk] = push(mine, mine, chunk * 6 + 3 + stage, axis)

    for copy in sent:
        copy.wait_send()
    sent.clear()

    def exchange(value, index):
        slot = turn_index * 2 + index
        tile[slot, 0] = jnp.broadcast_to(value, tile.shape[2:])
        copy = push(tile.at[slot, 0], tile.at[slot, 1], CHUNKS * 6 + index, 3)
        copy.wait_recv()
        return (tile[slot, 0] + tile[slot, 1])[:1, :1]

    def sweep(body):
        def step(index, carry):
            return carry + body(rows(index * STEP, STEP))

        lanes = lax.fori_loop(0, total // STEP, step, jnp.zeros((8, part.shape[1]), F32))
        return jnp.sum(lanes, keepdims=True)

    def fold(value):
        return jnp.sum(value.reshape(-1, 8, value.shape[1]), 0)

    if first:

        def copy_out(at):
            value = whole[at, :]
            direction[at, :] = value
            residual[at, :] = value
            answer[at, :] = jnp.zeros_like(value)
            return fold(value * value)

        norm[...] = jnp.broadcast_to(exchange(sweep(copy_out), 0), norm.shape)
    else:

        def meet(at):
            move = direction[at, :]
            image = whole[at, :] + SHIFT * move
            work[at, :] = image
            return fold(move * image)

        before = norm[:1, :1]
        alpha = before / exchange(sweep(meet), 0)

        def shrink(at):
            left = residual[at, :] - alpha * work[at, :]
            residual[at, :] = left
            answer[at, :] = answer[at, :] + alpha * direction[at, :]
            return fold(left * left)

        after = exchange(sweep(shrink), 1)
        beta = after / before

        def turn(index, carry):
            at = rows(index * STEP, STEP)
            direction[at, :] = residual[at, :] + beta * direction[at, :]
            return carry

        lax.fori_loop(0, total // STEP, turn, 0)
        norm[...] = jnp.broadcast_to(after, norm.shape)
    for copy in sent:
        copy.wait_send()


def whole_kernel(near_maps, samples, weight, own_info, kernel, tables, answer, residual, maps, info, data, arrived,
                 marks, back_high, back_low, middle, grid, grid_high, grid_low, part, direction, norm, whole, landed,
                 work, tile, map_send, map_recv, send, recv):
    slab, coil = lax.axis_index("slab"), lax.axis_index("coil")
    core, chip, far, near = coil % 2, coil // 2, slab // 2, slab % 2
    partners = (
        {"coil": chip * 2 + (1 - core)},
        {"coil": (1 - chip) * 2 + core},
        {"slab": (1 - far) * 2 + near},
        {"slab": far * 2 + (1 - near)},
        {"slab": (1 - far) * 2 + (1 - near)},
    )
    barrier = pltpu.get_barrier_semaphore()
    for partner in partners:
        pl.semaphore_signal(barrier, inc=1, device_id=partner, device_id_type=pl.DeviceIdType.MESH)
    pl.semaphore_wait(barrier, len(partners))
    space = (marks, back_high, back_low, middle, grid)
    sums = (part, direction, residual, answer, norm, whole, landed, work, tile, send, recv)
    adjoint_of_samples(near_maps, samples, weight, own_info, kernel, tables, part, maps, info, data, arrived,
                       *space, map_send, map_recv)
    combine(0, *sums)
    for step in range(ITERS):
        normal(direction, info, kernel, tables, maps, part, *space, grid_high, grid_low)
        combine(step + 1, *sums)


def whole_call(map_shape, tiles, slabs):
    coils, _, _, base, length = map_shape
    cells = RADIX * length
    rows = 2 * base * coils
    flat = (2 * RADIX * base, length)
    copies = (ITERS + 1) * (CHUNKS * 6 + 2)
    image = pltpu.VMEM(flat, F32)
    memory = pl.BlockSpec(memory_space=pltpu.VMEM)
    return pl.pallas_call(
        whole_kernel,
        out_shape=(jax.ShapeDtypeStruct(flat, F32), jax.ShapeDtypeStruct(flat, F32)),
        in_specs=[memory] * 6,
        out_specs=[memory] * 2,
        scratch_shapes=[
            pltpu.VMEM(map_shape, F32),
            pltpu.VMEM((8, tiles), F32),
            pltpu.VMEM((2, 2 * coils, tiles, base), F32),
            pltpu.VMEM((slabs, 8, tiles // slabs), F32),
            pltpu.VMEM((cells, tiles), BF16),
            pltpu.VMEM((rows, tiles), BF16),
            pltpu.VMEM((rows, tiles), BF16),
            pltpu.VMEM((RADIX, 2 * base, coils * length), F32),
            pltpu.VMEM((rows, cells), F32),
            pltpu.VMEM((rows, cells), BF16),
            pltpu.VMEM((rows, cells), BF16),
            image,
            image,
            pltpu.VMEM((8, 128), F32),
            image,
            pltpu.VMEM((CHUNKS, flat[0] // CHUNKS, length), F32),
            image,
            pltpu.VMEM((2 * ITERS + 2, 2, 8, 128), F32),
            pltpu.SemaphoreType.DMA((9,)),
            pltpu.SemaphoreType.DMA((9,)),
            pltpu.SemaphoreType.DMA((copies,)),
            pltpu.SemaphoreType.DMA((copies,)),
        ],
        compiler_params=pltpu.CompilerParams(
            collective_id=0, has_side_effects=True, vmem_limit_bytes=60 * 2**20
        ),
    )


def whole_coils(coil_maps, samples, kernel, tile_block, tile_count, dcf_level, dcf_table):
    ncoil, _, xpos, zdev, ylen = coil_maps.shape
    base = kernel.shape[0]
    slabs = lax.axis_size("slab")
    slab = lax.axis_index("slab")
    ky_dev = ylen // slabs
    lines = zdev // RADIX
    zblocks = zdev * slabs // base
    pairs = slabs // xpos
    group = ncoil // pairs

    near = coil_maps.reshape(pairs, group, 2, xpos, lines, RADIX, ylen).transpose(0, 1, 2, 3, 5, 4, 6)
    data = samples.reshape(ncoil * 2, *samples.shape[2:])
    shard_tiles = tile_block.shape[0]
    tiles = shard_tiles * slabs
    ky = slab * ky_dev + tile_block // zblocks % ky_dev
    column = tile_block % zblocks * ylen + ky % RADIX * base + ky // RADIX
    column = column + tile_block // (zblocks * ky_dev) * (zblocks * ylen)
    levels = jnp.arange(dcf_table.shape[0], dtype=jnp.int32)
    density = jnp.sum(jnp.where(dcf_level[:, None] == levels[None, :], dcf_table[None, :], 0.0), axis=1)
    position = jnp.arange(base, dtype=jnp.int32)
    weight = jnp.where(position[None, :] < tile_count[:, None], density[:, None], 0.0)
    info = jnp.stack((column.astype(F32), tile_count.astype(F32), density))
    info = jnp.concatenate((info, jnp.zeros((5, shard_tiles), F32)))

    tables = jnp.asarray(dft_tables(ylen))
    shape = (group, 2, RADIX, base, ylen)
    answer, residual = whole_call(shape, tiles, slabs)(near, data, weight, info, kernel, tables)

    both = jnp.stack((answer, residual)).reshape(2, 2, RADIX, base, ylen)
    partner = slab + 1 - 2 * (slab % 2)
    keep = lax.dynamic_slice_in_dim(both, slab * lines, lines, 3)
    give = lax.dynamic_slice_in_dim(both, partner * lines, lines, 3)
    core = lax.axis_index("coil") % 2
    swap = [(index, index ^ 1) for index in range(lax.axis_size("coil"))]
    half = lax.dynamic_index_in_dim(give, core, keepdims=False)
    half = lax.ppermute(half, "slab", [(index, index ^ 1) for index in range(slabs)])
    rest = lax.ppermute(half, "coil", swap)
    take = jnp.stack((jnp.where(core == 0, half, rest), jnp.where(core == 0, rest, half)))
    low = slab % 2 == 0
    both = jnp.stack((jnp.where(low, keep, take), jnp.where(low, take, keep)), 2)
    both = both.transpose(0, 1, 2, 4, 3, 5).reshape(2, 2, xpos, zdev, ylen)
    return both[0], both[1]


def fits(mesh, coil_maps, samples, kernel):
    slabs, coils = mesh.shape["slab"], mesh.shape["coil"]
    coil_dev = coil_maps.shape[0] // coils
    zlen, ylen = coil_maps.shape[3:]
    base = kernel.shape[0]
    return (
        coil_dev == slabs == coils == 4
        and coil_maps.shape[2] == 2
        and zlen == ylen == RADIX * base
        and base == 128
        and zlen % (slabs * RADIX) == 0
        and samples.shape[2] % 256 == 0
    )


def solution(mesh):
    placed = (
        P("coil", "scan", None, "slab", None),
        P("coil", "scan", "slab", None),
        P(),
        P("slab"),
        P("slab"),
        P("slab"),
        P(),
    )

    def run(coil_maps, samples, kernel, *rest):
        chosen = whole_coils if fits(mesh, coil_maps, samples, kernel) else body
        return jax.shard_map(
            chosen,
            mesh=mesh,
            in_specs=placed,
            out_specs=(P("scan", None, "slab", None), P("scan", None, "slab", None)),
            check_vma=False,
        )(coil_maps, samples, kernel, *rest)

    return run
```
